512 devices in a mesh: dp: 16 (over x, z_hi, core), seq: 32 (over y, z_lo).
Axes of the slice: x: 4, y: 4, z: 16 (z_hi: 2, z_lo: 8; z = z_hi * 8 + z_lo), core: 2. Of those that a mesh axis runs over, the one named last changes fastest.
Arguments:
- tokens: bfloat16 [16, 32, 128, 1152], P('dp', 'seq'), may hold values from -4 to 4
- spatial_qkv: bfloat16 [16, 32, 128, 3, 576], P('dp', 'seq'), may hold values from -8 to 8
- text_kv: bfloat16 [16, 128, 2, 576], P('dp'), may hold values from -6 to 6
- text_len: int32 [16], P('dp'), may hold values from 1 to 128
- w_os: bfloat16 [576, 1152], P('seq'), may hold values from -0.25 to 0.25
- w_qc: bfloat16 [1152, 576], P('seq'), may hold values from -0.1875 to 0.1875
- w_oc: bfloat16 [576, 1152], P('seq'), may hold values from -0.25 to 0.25
- w_qkv: bfloat16 [1152, 1728], P('seq'), may hold values from -0.1875 to 0.1875
- cotangent: bfloat16 [16, 32, 128, 576], P('dp', None, 'seq'), may hold values from -6 to 6
Outputs:
- temporal_heads: bfloat16 [16, 32, 128, 576], P('dp', None, 'seq')
- grad_tokens: bfloat16 [16, 32, 128, 1152], P('dp', 'seq')
- grad_qkv: bfloat16 [16, 32, 128, 3, 576], P('dp', 'seq')
- grad_os: float32 [576, 1152], P('seq')
The draws below stay inside these ranges and needn't reach their ends.
All inputs are finite; a program needn't handle non-finite values.
Results may differ from the reference program's by a relative error of at most 0.039.
Values may be sent and summed in bfloat16 or wider, within the bound.
A program may use at most 64 MiB of HBM per device.

```python
import math
import jax
import jax.numpy as jnp
from jax import lax

D = 1152
HEADS = 8
HEAD = 72
TEXT = 128
P_SIZE = 128
HD = 576
FRAMES = 32
CLIPS = 16


def draw_spatial_qkv(key, part):
    key = jax.random.fold_in(key, 11)
    full_shape = (CLIPS, FRAMES, P_SIZE, 3, HEADS * HEAD)
    return jnp.clip(jax.random.normal(key, full_shape, jnp.float32), -6.0, 6.0).astype(jnp.bfloat16)


def touch_ends(result, key, smallest, top_value):
    spot = [jax.random.randint(jax.random.fold_in(key, axis), (), 0, length) for axis, length in enumerate(result.shape)]
    widest = result.shape.index(max(result.shape))
    neighbour = spot[:widest] + [(spot[widest] + 1) % result.shape[widest]] + spot[widest + 1:]
    return result.at[tuple(spot)].set(smallest).at[tuple(neighbour)].set(top_value)


def block_levels(stream_key, shape, split, smallest, top_value):
    def one(dim, parts):
        steps = jax.random.uniform(jax.random.fold_in(jax.random.fold_in(stream_key, 6), dim), (parts,), jnp.float32, smallest / len(split), top_value / len(split))
        return jnp.repeat(jnp.exp(steps), shape[dim] // parts).reshape((-1,) + (1,) * (len(shape) - dim - 1))

    level = one(*split[0])
    for cut in split[1:]:
        level = level * one(*cut)
    return level


def noise(key, dims, width, most, split=(), dtype=jnp.bfloat16):
    values = width * jax.random.normal(key, dims, jnp.float32)
    if split:
        values = values * block_levels(key, dims, split, -0.22, 0.18)
    return jnp.clip(values, -most, most).astype(dtype)


def setup_inputs(seed: int = 0) -> dict:
    streams_of = jax.random.split(jax.random.key(seed), 10)
    tokens = noise(streams_of[0], (CLIPS, FRAMES, P_SIZE, D), 0.5, 4.0, ((0, 16), (1, 32)))
    spatial_qkv = draw_spatial_qkv(jax.random.fold_in(streams_of[9], 71), 0)
    text_kv = noise(streams_of[2], (CLIPS, TEXT, 2, HD), 1.0, 6.0, ((0, 16),))
    text_len = touch_ends(jax.random.randint(streams_of[3], (CLIPS,), 1, TEXT + 1), jax.random.fold_in(streams_of[3], 1), 1, TEXT).astype(jnp.int32)
    w_os = noise(streams_of[4], (HD, D), HD ** -0.5, 0.25, ((0, 32),))
    w_qc = noise(streams_of[5], (D, HD), D ** -0.5, 0.1875, ((0, 32),))
    w_oc = noise(streams_of[6], (HD, D), HD ** -0.5, 0.25, ((0, 32),))
    w_qkv = noise(streams_of[7], (D, 3 * HD), D ** -0.5, 0.1875, ((0, 32),))
    cotangent = noise(streams_of[8], (CLIPS, FRAMES, P_SIZE, HD), 1.0, 6.0, ((0, 16), (2, 32)))
    return {"tokens": tokens, "spatial_qkv": spatial_qkv, "text_kv": text_kv, "text_len": text_len, "w_os": w_os, "w_qc": w_qc, "w_oc": w_oc, "w_qkv": w_qkv, "cotangent": cotangent}


def rounded(array):
    return lax.optimization_barrier(array.astype(jnp.bfloat16)).astype(jnp.float32)

def split_heads(array):
    return array.reshape(array.shape[:-1] + (HEADS, HEAD))

def join_heads(array):
    return array.reshape(array.shape[:-2] + (HEADS * HEAD,))

def attend(queries, key_rows, values, score_scale, visible):
    scores = jnp.einsum('...qhe,...khe->...hqk', queries.astype(jnp.float32), key_rows.astype(jnp.float32)) * score_scale
    if visible is not None:
        scores = jnp.where(visible, scores, -1e+30)
    weights = jax.nn.softmax(scores, axis=-1)
    output = jnp.einsum('...hqk,...khe->...qhe', rounded(weights), values.astype(jnp.float32))
    return (output.astype(jnp.bfloat16), weights)

def attend_grad(upstream, queries, key_rows, values, weights, score_scale, with_memory):
    upper = upstream.astype(jnp.float32)
    prob_grad = jnp.einsum('...qhe,...khe->...hqk', upper, values.astype(jnp.float32))
    score_grad = rounded(weights * (prob_grad - lax.optimization_barrier(jnp.sum(prob_grad * weights, axis=-1, keepdims=True))))
    query_grad = (score_scale * jnp.einsum('...hqk,...khe->...qhe', score_grad, key_rows.astype(jnp.float32))).astype(jnp.bfloat16)
    if not with_memory:
        return query_grad
    value_grad = jnp.einsum('...hqk,...qhe->...khe', rounded(weights), upper).astype(jnp.bfloat16)
    key_grad = (score_scale * jnp.einsum('...hqk,...qhe->...khe', score_grad, queries.astype(jnp.float32))).astype(jnp.bfloat16)
    return (query_grad, key_grad, value_grad)

def reference(tokens, spatial_qkv, text_kv, text_len, w_os, w_qc, w_oc, w_qkv, cotangent):
    score_scale = 1.0 / math.sqrt(HEAD)
    inner = HEADS * HEAD

    def one_clip(inputs):
        clip_tokens, clip_qkv, clip_text, clip_len, clip_cot = inputs
        row_count = FRAMES * P_SIZE
        spatial = split_heads(clip_qkv)
        spatial_out, spatial_weights = attend(spatial[:, :, 0], spatial[:, :, 1], spatial[:, :, 2], score_scale, None)
        mixed = join_heads(spatial_out).reshape(row_count, inner)
        hidden = (clip_tokens.reshape(row_count, D).astype(jnp.float32) + jnp.dot(mixed, w_os, preferred_element_type=jnp.float32)).astype(jnp.bfloat16)
        cross_queries = split_heads(jnp.dot(hidden, w_qc, preferred_element_type=jnp.float32).astype(jnp.bfloat16))
        text_keys = split_heads(clip_text[:, 0])
        text_values = split_heads(clip_text[:, 1])
        visible = jnp.arange(TEXT) < clip_len
        cross_out, cross_weights = attend(cross_queries, text_keys, text_values, score_scale, visible)
        after = (hidden.astype(jnp.float32) + jnp.dot(join_heads(cross_out), w_oc, preferred_element_type=jnp.float32)).astype(jnp.bfloat16)
        projected = jnp.dot(after, w_qkv, preferred_element_type=jnp.float32).astype(jnp.bfloat16)
        temporal = jnp.swapaxes(split_heads(projected.reshape(FRAMES, P_SIZE, 3, inner)), 0, 1)
        temporal_out, temporal_weights = attend(temporal[:, :, 0], temporal[:, :, 1], temporal[:, :, 2], score_scale, None)
        temporal_heads = jnp.swapaxes(join_heads(temporal_out), 0, 1)
        upstream = split_heads(jnp.swapaxes(clip_cot, 0, 1))
        grads = attend_grad(upstream, temporal[:, :, 0], temporal[:, :, 1], temporal[:, :, 2], temporal_weights, score_scale, True)
        proj_grad = jnp.swapaxes(jnp.stack(grads, axis=2), 0, 1).reshape(row_count, 3 * inner)
        after_grad = jnp.dot(proj_grad, w_qkv.T, preferred_element_type=jnp.float32).astype(jnp.bfloat16)
        cross_grad = split_heads(jnp.dot(after_grad, w_oc.T, preferred_element_type=jnp.float32).astype(jnp.bfloat16))
        cross_query_grad = attend_grad(cross_grad, cross_queries, text_keys, text_values, cross_weights, score_scale, False)
        hidden_grad = (after_grad.astype(jnp.float32) + jnp.dot(join_heads(cross_query_grad), w_qc.T, preferred_element_type=jnp.float32)).astype(jnp.bfloat16)
        mixed_grad = jnp.dot(hidden_grad, w_os.T, preferred_element_type=jnp.float32).astype(jnp.bfloat16)
        partial_grad = jnp.dot(mixed.T, hidden_grad, preferred_element_type=jnp.float32)
        spatial_grads = attend_grad(split_heads(mixed_grad.reshape(FRAMES, P_SIZE, inner)), spatial[:, :, 0], spatial[:, :, 1], spatial[:, :, 2], spatial_weights, score_scale, True)
        qkv_grad = join_heads(jnp.stack(spatial_grads, axis=2))
        return (temporal_heads, hidden_grad.reshape(FRAMES, P_SIZE, D), qkv_grad, partial_grad)
    heads_all, tokens_grad, qkv_grad, partials = lax.map(one_clip, (tokens, spatial_qkv, text_kv, text_len, cotangent))
    return (heads_all, tokens_grad, qkv_grad, lax.optimization_barrier(jnp.sum(partials, axis=0)))
```

```python
import functools
import math

import jax
import jax.numpy as jnp
from jax import lax
from jax.experimental import pallas as pl
from jax.experimental.pallas import tpu as pltpu
from jax.sharding import PartitionSpec as P

HEADS = 8
HEAD = 72
MESH = pl.DeviceIdType.MESH
BF16 = jnp.bfloat16
F32 = jnp.float32
SHARDS = ((18, 32, 1152, 80), (36, 48, 576, 144), (18, 32, 1152, 80), (36, 48, 1728, 144))


def place():
    dp, seq = lax.axis_index("dp"), lax.axis_index("seq")
    return lax.rem(dp, 2), lax.div(dp, 4), lax.div(seq, 8), lax.rem(lax.div(dp, 2), 2) * 8 + lax.rem(seq, 8)


def device(core, x, y, z):
    return ((x * 2 + lax.div(z, 8)) * 2 + core, y * 8 + lax.rem(z, 8))


class Gather:
    def __init__(self, shards, landing, full, sems):
        self.shards, self.landing, self.full = shards, landing, full
        (self.zs, self.zr, self.ps, self.pr, self.ys, self.yr, self.qs, self.qr) = sems
        core, x, y, z = place()
        self.core, self.y, self.slot = core, y, lax.rem(z, 8)
        self.step = 1 - 2 * core
        self.next_z = device(core, x, y, lax.rem(z + self.step + 16, 16))
        self.prev_z = device(core, x, y, lax.rem(z - self.step + 16, 16))
        self.next_y = device(core, x, lax.rem(y + self.step + 4, 4), z)
        self.prev_y = device(core, x, lax.rem(y - self.step + 4, 4), z)
        self.partner = device(1 - core, x, y, z)

    def neighbours(self):
        return (self.next_z, self.prev_z, self.next_y, self.prev_y, self.partner)

    def stage(self, w):
        rows = SHARDS[w][0]
        block = self.landing[w]
        block[self.slot] = jnp.zeros(block.shape[1:], BF16)
        block[self.slot, 0:rows, :] = self.shards[w][...]

    def z_copy(self, w, s, slot):
        block = self.landing[w].at[slot]
        return pltpu.make_async_remote_copy(
            src_ref=block, dst_ref=block, send_sem=self.zs.at[w, s], recv_sem=self.zr.at[w, s],
            device_id=self.next_z, device_id_type=MESH)

    def pass_copy(self, w, s, slot):
        block = self.landing[w].at[slot]
        return pltpu.make_async_remote_copy(
            src_ref=block, dst_ref=block, send_sem=self.ps.at[w, s], recv_sem=self.pr.at[w, s],
            device_id=self.partner, device_id_type=MESH)

    def away(self, steps):
        return lax.rem(self.slot - steps * self.step + 8, 8)

    def z_start(self, w):
        self.z_copy(w, 0, self.slot).start()

    def z_step(self, w, s):
        def go():
            slot = self.away(s + 1)
            self.z_copy(w, s, slot).wait_recv()
            if s < 2:
                self.z_copy(w, s + 1, slot).start()
            if s == 2:
                pl.when(self.core == 0)(lambda: self.z_copy(w, 3, slot).start())
            self.pass_copy(w, s, slot).start()

        if s < 3:
            go()
        else:
            pl.when(self.core == 0)(go)

    def z_finish(self, w):
        for s in range(3):
            self.pass_copy(w, s, lax.rem(self.slot + (s + 1) * self.step + 8, 8)).wait_recv()
        pl.when(self.core == 1)(
            lambda: self.pass_copy(w, 3, lax.rem(self.slot + 4, 8)).wait_recv())
        rows = SHARDS[w][0]
        for k in range(8):
            self.full[w][self.y, k * rows:(k + 1) * rows, :] = self.landing[w][k, 0:rows, :]

    def y_copy(self, w, s, quarter, part, to, send, recv):
        block = self.full[w].at[quarter] if part is None else self.full[w].at[quarter, pl.ds(*part)]
        return pltpu.make_async_remote_copy(
            src_ref=block, dst_ref=block, send_sem=send.at[w, s], recv_sem=recv.at[w, s],
            device_id=to, device_id_type=MESH)

    def parts(self, w):
        cut, rows = SHARDS[w][3], SHARDS[w][0] * 8
        return ((0, cut), (cut, rows - cut))

    def y_start(self, w):
        self.y_copy(w, 0, self.y, None, self.next_y, self.ys, self.yr).start()

    def y_step(self, w):
        quarter = lax.rem(self.y - self.step + 4, 4)
        self.y_copy(w, 0, quarter, None, self.next_y, self.ys, self.yr).wait_recv()
        for c in range(2):
            pl.when(self.core == c)(
                lambda: self.y_copy(w, 1, quarter, self.parts(w)[c], self.next_y, self.ys, self.yr).start())
        self.y_copy(w, 0, quarter, None, self.partner, self.qs, self.qr).start()

    def y_last(self, w):
        quarter = lax.rem(self.y + 2, 4)
        for c in range(2):
            def go():
                self.y_copy(w, 1, quarter, self.parts(w)[c], self.next_y, self.ys, self.yr).wait_recv()
                self.y_copy(w, 1, quarter, self.parts(w)[c], self.partner, self.qs, self.qr).start()
            pl.when(self.core == c)(go)

    def y_finish(self, w):
        quarter = lax.rem(self.y + self.step + 4, 4)
        self.y_copy(w, 0, quarter, None, self.partner, self.qs, self.qr).wait_recv()
        far = lax.rem(self.y + 2, 4)
        for c in range(2):
            pl.when(self.core == c)(
                lambda: self.y_copy(w, 1, far, self.parts(w)[1 - c], self.partner, self.qs, self.qr).wait_recv())

    def drain(self, w):
        for s in range(3):
            self.z_copy(w, s, self.away(s)).wait_send()
            self.pass_copy(w, s, self.away(s + 1)).wait_send()

        def last():
            self.z_copy(w, 3, self.away(3)).wait_send()
            self.pass_copy(w, 3, self.away(4)).wait_send()

        pl.when(self.core == 0)(last)
        self.y_copy(w, 0, self.y, None, self.next_y, self.ys, self.yr).wait_send()
        quarter = lax.rem(self.y - self.step + 4, 4)
        self.y_copy(w, 0, quarter, None, self.partner, self.qs, self.qr).wait_send()
        far = lax.rem(self.y + 2, 4)
        for c in range(2):
            def go():
                self.y_copy(w, 1, quarter, self.parts(w)[c], self.next_y, self.ys, self.yr).wait_send()
                self.y_copy(w, 1, far, self.parts(w)[c], self.partner, self.qs, self.qr).wait_send()
            pl.when(self.core == c)(go)


def gather_kernel(*refs):
    shards, full, landing, sems = refs[0:4], refs[4:8], refs[8:12], refs[12:20]
    g = Gather(shards, landing, full, sems)
    barrier = pltpu.get_barrier_semaphore()
    for d in g.neighbours():
        pl.semaphore_signal(barrier, inc=1, device_id=d, device_id_type=MESH)
    for w in range(4):
        g.stage(w)
    pl.semaphore_wait(barrier, 5)
    first = (0, 1, 2)
    for w in first:
        g.z_start(w)
    for s in range(4):
        for w in first:
            g.z_step(w, s)
    g.z_start(3)
    for w in first:
        g.z_finish(w)
        g.y_start(w)
    for s in range(4):
        g.z_step(3, s)
        if s < 3:
            g.y_step(s)
    g.z_finish(3)
    g.y_start(3)
    for w in first:
        g.y_last(w)
    for w in first:
        g.y_finish(w)
    g.y_step(3)
    g.y_last(3)
    g.y_finish(3)
    for w in range(4):
        g.drain(w)


def gather_weights(*shards):
    vmem = pl.BlockSpec(memory_space=pltpu.VMEM)
    out = pl.pallas_call(
        gather_kernel,
        out_shape=[jax.ShapeDtypeStruct((4, rows * 8, columns), BF16) for rows, _, columns, _ in SHARDS],
        in_specs=[vmem] * 4,
        out_specs=[vmem] * 4,
        scratch_shapes=[pltpu.VMEM((8, padded, columns), BF16) for _, padded, columns, _ in SHARDS]
        + [pltpu.SemaphoreType.DMA((4, 4))] * 4 + [pltpu.SemaphoreType.DMA((4, 2))] * 4,
        compiler_params=pltpu.CompilerParams(
            collective_id=0, has_side_effects=True, vmem_limit_bytes=48 * 2**20),
        name="gather_weights",
    )(*shards)
    return [o.reshape(-1, o.shape[-1]) for o in out]


def split_heads(array):
    return array.reshape(array.shape[:-1] + (HEADS, HEAD))


def join_heads(array):
    return array.reshape(array.shape[:-2] + (HEADS * HEAD,))


def times_transposed(left, right):
    return lax.dot_general(
        left, right, (((1,), (1,)), ((), ())), preferred_element_type=jnp.float32
    )


def attend(queries, key_rows, values, score_scale, visible):
    scores = (
        jnp.einsum("bqhe,bkhe->bhqk", queries, key_rows, preferred_element_type=jnp.float32)
        * score_scale
    )
    if visible is not None:
        scores = jnp.where(visible, scores, -1e30)
    weights = jax.nn.softmax(scores, axis=-1)
    output = jnp.einsum(
        "bhqk,bkhe->bqhe", weights.astype(jnp.bfloat16), values, preferred_element_type=jnp.float32
    )
    return (output.astype(jnp.bfloat16), weights)


def attend_grad(upstream, queries, key_rows, values, weights, score_scale, with_memory):
    prob_grad = jnp.einsum("bqhe,bkhe->bhqk", upstream, values, preferred_element_type=jnp.float32)
    score_grad = (
        weights * (prob_grad - jnp.sum(prob_grad * weights, axis=-1, keepdims=True))
    ).astype(jnp.bfloat16)
    query_grad = (
        score_scale
        * jnp.einsum("bhqk,bkhe->bqhe", score_grad, key_rows, preferred_element_type=jnp.float32)
    ).astype(jnp.bfloat16)
    if not with_memory:
        return query_grad
    value_grad = jnp.einsum(
        "bhqk,bqhe->bkhe",
        weights.astype(jnp.bfloat16),
        upstream,
        preferred_element_type=jnp.float32,
    ).astype(jnp.bfloat16)
    key_grad = (
        score_scale
        * jnp.einsum("bhqk,bqhe->bkhe", score_grad, queries, preferred_element_type=jnp.float32)
    ).astype(jnp.bfloat16)
    return (query_grad, key_grad, value_grad)


def shards(tokens, spatial_qkv, text_kv, text_len, w_os, w_qc, w_oc, w_qkv, cotangent):
    frame_count, patch_count, model_width = (tokens.shape[1], tokens.shape[2], tokens.shape[3])
    inner = HEADS * HEAD
    row_count = frame_count * patch_count
    score_scale = 1.0 / math.sqrt(HEAD)
    full_os, full_qc, full_oc, full_qkv = gather_weights(w_os, w_qc, w_oc, w_qkv)
    spatial = split_heads(spatial_qkv[0])
    spatial_queries, spatial_keys, spatial_values = (
        spatial[:, :, 0],
        spatial[:, :, 1],
        spatial[:, :, 2],
    )
    spatial_out, spatial_weights = attend(
        spatial_queries, spatial_keys, spatial_values, score_scale, None
    )
    mixed = join_heads(spatial_out).reshape(row_count, inner)
    hidden = (
        tokens[0].reshape(row_count, model_width).astype(jnp.float32)
        + jnp.dot(mixed, full_os, preferred_element_type=jnp.float32)
    ).astype(jnp.bfloat16)
    cross_queries = split_heads(
        jnp.dot(hidden, full_qc, preferred_element_type=jnp.float32).astype(jnp.bfloat16)
    )[None]
    text_keys = split_heads(text_kv[0, :, 0])[None]
    text_values = split_heads(text_kv[0, :, 1])[None]
    visible = jnp.arange(text_kv.shape[1]) < text_len[0]
    cross_out, cross_weights = attend(cross_queries, text_keys, text_values, score_scale, visible)
    after = (
        hidden.astype(jnp.float32)
        + jnp.dot(join_heads(cross_out[0]), full_oc, preferred_element_type=jnp.float32)
    ).astype(jnp.bfloat16)
    patched = lax.all_to_all(
        after.reshape(frame_count, patch_count, model_width),
        "seq",
        split_axis=1,
        concat_axis=0,
        tiled=True,
    )
    all_frames, local_patches = (patched.shape[0], patched.shape[1])
    flat_patched = patched.reshape(all_frames * local_patches, model_width)
    projected = jnp.dot(flat_patched, full_qkv, preferred_element_type=jnp.float32)
    temporal = jnp.swapaxes(
        split_heads(projected.astype(jnp.bfloat16).reshape(all_frames, local_patches, 3, inner)),
        0,
        1,
    )
    temporal_queries, temporal_keys, temporal_values = (
        temporal[:, :, 0],
        temporal[:, :, 1],
        temporal[:, :, 2],
    )
    temporal_out, temporal_weights = attend(
        temporal_queries, temporal_keys, temporal_values, score_scale, None
    )
    temporal_heads = jnp.swapaxes(join_heads(temporal_out), 0, 1)[None]
    upstream = split_heads(jnp.swapaxes(cotangent[0], 0, 1))
    temporal_grads = attend_grad(
        upstream,
        temporal_queries,
        temporal_keys,
        temporal_values,
        temporal_weights,
        score_scale,
        True,
    )
    proj_grad = jnp.swapaxes(jnp.stack(temporal_grads, axis=2), 0, 1).reshape(
        all_frames * local_patches, 3 * inner
    )
    patch_grad = times_transposed(proj_grad, full_qkv)
    patch_grad = patch_grad.astype(jnp.bfloat16).reshape(all_frames, local_patches, model_width)
    after_grad = lax.all_to_all(patch_grad, "seq", split_axis=0, concat_axis=1, tiled=True).reshape(
        row_count, model_width
    )
    cross_grad = split_heads(times_transposed(after_grad, full_oc).astype(jnp.bfloat16))[None]
    cross_query_grad = attend_grad(
        cross_grad, cross_queries, text_keys, text_values, cross_weights, score_scale, False
    )
    hidden_grad = (
        after_grad.astype(jnp.float32) + times_transposed(join_heads(cross_query_grad[0]), full_qc)
    ).astype(jnp.bfloat16)
    mixed_grad = times_transposed(hidden_grad, full_os).astype(jnp.bfloat16)
    partial_grad = lax.dot_general(
        mixed, hidden_grad, (((0,), (0,)), ((), ())), preferred_element_type=jnp.float32
    )
    grad_share = lax.psum_scatter(
        partial_grad.astype(jnp.bfloat16), "seq", scatter_dimension=0, tiled=True
    )
    grad_os = lax.psum(grad_share, "dp").astype(jnp.float32)
    spatial_grads = attend_grad(
        split_heads(mixed_grad.reshape(frame_count, patch_count, inner)),
        spatial_queries,
        spatial_keys,
        spatial_values,
        spatial_weights,
        score_scale,
        True,
    )
    qkv_grad = join_heads(jnp.stack(spatial_grads, axis=2))[None]
    return (
        temporal_heads,
        hidden_grad.reshape(1, frame_count, patch_count, model_width),
        qkv_grad,
        grad_os,
    )


def solution(mesh):
    placed = (
        P("dp", "seq", None, None),
        P("dp", "seq", None, None, None),
        P("dp", None, None, None),
        P("dp"),
        P("seq", None),
        P("seq", None),
        P("seq", None),
        P("seq", None),
        P("dp", None, "seq", None),
    )
    return jax.shard_map(
        shards,
        mesh=mesh,
        in_specs=placed,
        out_specs=(
            P("dp", None, "seq", None),
            P("dp", "seq", None, None),
            P("dp", "seq", None, None, None),
            P("seq", None),
        ),
        check_vma=False,
    )
```

```python
import functools
import math

import jax
import jax.numpy as jnp
from jax import lax
from jax.experimental import pallas as pl
from jax.experimental.pallas import tpu as pltpu
from jax.sharding import PartitionSpec as P

HEADS = 8
HEAD = 72
MESH = pl.DeviceIdType.MESH
BF16 = jnp.bfloat16
F32 = jnp.float32
SHARDS = ((18, 32, 1152, 80), (36, 48, 576, 144), (18, 32, 1152, 80), (36, 48, 1728, 144))


def place():
    dp, seq = lax.axis_index("dp"), lax.axis_index("seq")
    return lax.rem(dp, 2), lax.div(dp, 4), lax.div(seq, 8), lax.rem(lax.div(dp, 2), 2) * 8 + lax.rem(seq, 8)


def device(core, x, y, z):
    return ((x * 2 + lax.div(z, 8)) * 2 + core, y * 8 + lax.rem(z, 8))


class Gather:
    def __init__(self, shards, landing, full, sems):
        self.shards, self.landing, self.full = shards, landing, full
        (self.zs, self.zr, self.ps, self.pr, self.ys, self.yr, self.qs, self.qr) = sems
        core, x, y, z = place()
        self.core, self.y, self.slot = core, y, lax.rem(z, 8)
        self.step = 1 - 2 * core
        self.next_z = device(core, x, y, lax.rem(z + self.step + 16, 16))
        self.prev_z = device(core, x, y, lax.rem(z - self.step + 16, 16))
        self.next_y = device(core, x, lax.rem(y + self.step + 4, 4), z)
        self.prev_y = device(core, x, lax.rem(y - self.step + 4, 4), z)
        self.partner = device(1 - core, x, y, z)

    def neighbours(self):
        return (self.next_z, self.prev_z, self.next_y, self.prev_y, self.partner)

    def stage(self, w):
        rows = SHARDS[w][0]
        block = self.landing[w]
        block[self.slot] = jnp.zeros(block.shape[1:], BF16)
        block[self.slot, 0:rows, :] = self.shards[w][...]

    def z_copy(self, w, s, slot):
        block = self.landing[w].at[slot]
        return pltpu.make_async_remote_copy(
            src_ref=block, dst_ref=block, send_sem=self.zs.at[w, s], recv_sem=self.zr.at[w, s],
            device_id=self.next_z, device_id_type=MESH)

    def pass_copy(self, w, s, slot):
        block = self.landing[w].at[slot]
        return pltpu.make_async_remote_copy(
            src_ref=block, dst_ref=block, send_sem=self.ps.at[w, s], recv_sem=self.pr.at[w, s],
            device_id=self.partner, device_id_type=MESH)

    def away(self, steps):
        return lax.rem(self.slot - steps * self.step + 8, 8)

    def z_start(self, w):
        self.z_copy(w, 0, self.slot).start()

    def z_step(self, w, s):
        def go():
            slot = self.away(s + 1)
            self.z_copy(w, s, slot).wait_recv()
            if s < 2:
                self.z_copy(w, s + 1, slot).start()
            if s == 2:
                pl.when(self.core == 0)(lambda: self.z_copy(w, 3, slot).start())
            self.pass_copy(w, s, slot).start()

        if s < 3:
            go()
        else:
            pl.when(self.core == 0)(go)

    def z_finish(self, w):
        for s in range(3):
            self.pass_copy(w, s, lax.rem(self.slot + (s + 1) * self.step + 8, 8)).wait_recv()
        pl.when(self.core == 1)(
            lambda: self.pass_copy(w, 3, lax.rem(self.slot + 4, 8)).wait_recv())
        rows = SHARDS[w][0]
        for k in range(8):
            self.full[w][self.y, k * rows:(k + 1) * rows, :] = self.landing[w][k, 0:rows, :]

    def y_copy(self, w, s, quarter, part, to, send, recv):
        block = self.full[w].at[quarter] if part is None else self.full[w].at[quarter, pl.ds(*part)]
        return pltpu.make_async_remote_copy(
            src_ref=block, dst_ref=block, send_sem=send.at[w, s], recv_sem=recv.at[w, s],
            device_id=to, device_id_type=MESH)

    def parts(self, w):
        cut, rows = SHARDS[w][3], SHARDS[w][0] * 8
        return ((0, cut), (cut, rows - cut))

    def y_start(self, w):
        self.y_copy(w, 0, self.y, None, self.next_y, self.ys, self.yr).start()

    def y_step(self, w):
        quarter = lax.rem(self.y - self.step + 4, 4)
        self.y_copy(w, 0, quarter, None, self.next_y, self.ys, self.yr).wait_recv()
        for c in range(2):
            pl.when(self.core == c)(
                lambda: self.y_copy(w, 1, quarter, self.parts(w)[c], self.next_y, self.ys, self.yr).start())
        self.y_copy(w, 0, quarter, None, self.partner, self.qs, self.qr).start()

    def y_last(self, w):
        quarter = lax.rem(self.y + 2, 4)
        for c in range(2):
            def go():
                self.y_copy(w, 1, quarter, self.parts(w)[c], self.next_y, self.ys, self.yr).wait_recv()
                self.y_copy(w, 1, quarter, self.parts(w)[c], self.partner, self.qs, self.qr).start()
            pl.when(self.core == c)(go)

    def y_finish(self, w):
        quarter = lax.rem(self.y + self.step + 4, 4)
        self.y_copy(w, 0, quarter, None, self.partner, self.qs, self.qr).wait_recv()
        far = lax.rem(self.y + 2, 4)
        for c in range(2):
            pl.when(self.core == c)(
                lambda: self.y_copy(w, 1, far, self.parts(w)[1 - c], self.partner, self.qs, self.qr).wait_recv())

    def drain(self, w):
        for s in range(3):
            self.z_copy(w, s, self.away(s)).wait_send()
            self.pass_copy(w, s, self.away(s + 1)).wait_send()

        def last():
            self.z_copy(w, 3, self.away(3)).wait_send()
            self.pass_copy(w, 3, self.away(4)).wait_send()

        pl.when(self.core == 0)(last)
        self.y_copy(w, 0, self.y, None, self.next_y, self.ys, self.yr).wait_send()
        quarter = lax.rem(self.y - self.step + 4, 4)
        self.y_copy(w, 0, quarter, None, self.partner, self.qs, self.qr).wait_send()
        far = lax.rem(self.y + 2, 4)
        for c in range(2):
            def go():
                self.y_copy(w, 1, quarter, self.parts(w)[c], self.next_y, self.ys, self.yr).wait_send()
                self.y_copy(w, 1, far, self.parts(w)[c], self.partner, self.qs, self.qr).wait_send()
            pl.when(self.core == c)(go)


def gather_kernel(*refs):
    shards, full, landing, sems = refs[0:4], refs[4:8], refs[8:12], refs[12:20]
    g = Gather(shards, landing, full, sems)
    barrier = pltpu.get_barrier_semaphore()
    for d in g.neighbours():
        pl.semaphore_signal(barrier, inc=1, device_id=d, device_id_type=MESH)
    for w in range(4):
        g.stage(w)
    pl.semaphore_wait(barrier, 5)
    first = (0, 1, 2)
    for w in first:
        g.z_start(w)
    for s in range(4):
        for w in first:
            g.z_step(w, s)
    g.z_start(3)
    for w in first:
        g.z_finish(w)
        g.y_start(w)
    for s in range(4):
        g.z_step(3, s)
        if s < 3:
            g.y_step(s)
    g.z_finish(3)
    g.y_start(3)
    for w in first:
        g.y_last(w)
    for w in first:
        g.y_finish(w)
    g.y_step(3)
    g.y_last(3)
    g.y_finish(3)
    for w in range(4):
        g.drain(w)


def gather_weights(*shards):
    vmem = pl.BlockSpec(memory_space=pltpu.VMEM)
    out = pl.pallas_call(
        gather_kernel,
        out_shape=[jax.ShapeDtypeStruct((4, rows * 8, columns), BF16) for rows, _, columns, _ in SHARDS],
        in_specs=[vmem] * 4,
        out_specs=[vmem] * 4,
        scratch_shapes=[pltpu.VMEM((8, padded, columns), BF16) for _, padded, columns, _ in SHARDS]
        + [pltpu.SemaphoreType.DMA((4, 4))] * 4 + [pltpu.SemaphoreType.DMA((4, 2))] * 4,
        compiler_params=pltpu.CompilerParams(
            collective_id=0, has_side_effects=True, vmem_limit_bytes=48 * 2**20),
        name="gather_weights",
    )(*shards)
    return [o.reshape(-1, o.shape[-1]) for o in out]


class Reduce:
    def __init__(self, partial, taken, pieces, plane, total, z_out, z_in, x_out, x_in, sems):
        self.partial, self.taken, self.pieces, self.plane = partial, taken, pieces, plane
        self.total, self.z_out, self.z_in, self.x_out, self.x_in = total, z_out, z_in, x_out, x_in
        (self.cs, self.cr, self.ps, self.pr, self.zs, self.zr, self.xs, self.xr) = sems
        self.core, self.x, self.y, self.z = place()
        self.holds = jnp.logical_and(self.x < 3, lax.div(self.y, 2) == self.core)
        self.me = self.x * 4 + self.y

    def greet(self, barrier):
        def signal(d):
            pl.semaphore_signal(barrier, inc=1, device_id=d, device_id_type=MESH)

        core, x, y, z = self.core, self.x, self.y, self.z

        @pl.loop(1, 16)
        def _(k):
            signal(device(core, lax.rem(x + lax.div(k, 4), 4), lax.rem(y + lax.rem(k, 4), 4), z))
            signal(device(core, x, y, lax.rem(z + k, 16)))

        @pl.loop(0, 4)
        def _(k):
            signal(device(1 - core, lax.rem(x + k, 4), y, z))

        return 34

    def core_copy(self):
        return pltpu.make_async_remote_copy(
            src_ref=self.partial.at[1 - self.core], dst_ref=self.taken, send_sem=self.cs, recv_sem=self.cr,
            device_id=device(1 - self.core, self.x, self.y, self.z), device_id_type=MESH)

    def plane_copy(self, upper, x):
        return pltpu.make_async_remote_copy(
            src_ref=self.pieces.at[upper, x], dst_ref=self.plane.at[self.me],
            send_sem=self.ps.at[upper * 3 + x], recv_sem=self.pr.at[self.me],
            device_id=device(self.core, x, self.core * 2 + upper, self.z), device_id_type=MESH)

    def is_me(self, upper, x):
        return jnp.logical_and(self.x == x, self.y == self.core * 2 + upper)

    def plane_start(self):
        self.core_copy().wait_recv()
        for upper in range(2):
            for x in range(3):
                rows, columns = slice(144 * upper, 144 * upper + 144), slice(384 * x, 384 * x + 384)
                self.pieces[upper, x] = (
                    self.partial[self.core, rows, columns].astype(F32)
                    + self.taken[rows, columns].astype(F32)).astype(BF16)
        for upper in range(2):
            for x in range(3):
                pl.when(jnp.logical_not(self.is_me(upper, x)))(
                    lambda: self.plane_copy(upper, x).start())

                @pl.when(self.is_me(upper, x))
                def _():
                    self.plane[self.me] = self.pieces[upper, x]

    def z_copy(self, k):
        to = lax.rem(self.z + k, 16)
        return pltpu.make_async_remote_copy(
            src_ref=self.z_out.at[lax.rem(to, 8)], dst_ref=self.z_in.at[self.z],
            send_sem=self.zs.at[k], recv_sem=self.zr.at[self.z],
            device_id=device(self.core, self.x, self.y, to), device_id_type=MESH)

    def z_start(self):
        @pl.when(self.holds)
        def _():
            @pl.loop(0, 16)
            def _(k):
                @pl.when(k != self.me)
                def _():
                    block = self.plane.at[k]
                    pltpu.make_async_remote_copy(
                        src_ref=block, dst_ref=block, send_sem=self.ps.at[0], recv_sem=self.pr.at[k],
                        device_id=device(1 - self.core, self.x, self.y, self.z), device_id_type=MESH).wait_recv()

            for r in range(3):
                rows = slice(48 * r, 48 * r + 48)
                sum_rows = self.plane[0, rows].astype(F32)
                for k in range(1, 16):
                    sum_rows = sum_rows + self.plane[k, rows].astype(F32)
                self.total[rows] = sum_rows
            self.z_out[...] = jnp.zeros(self.z_out.shape, BF16)
            for k in range(8):
                self.z_out[k, 0:18, :] = self.total[18 * k:18 * k + 18, :].astype(BF16)

            @pl.loop(1, 16)
            def _(k):
                self.z_copy(k).start()

            self.z_in[self.z] = self.z_out[lax.rem(self.z, 8)]

    def x_copy(self, k):
        other = lax.div(k, 4)
        return pltpu.make_async_remote_copy(
            src_ref=self.x_out, dst_ref=self.x_in.at[self.x],
            send_sem=self.xs.at[k], recv_sem=self.xr.at[self.x],
            device_id=device(lax.rem(self.core + other, 2), lax.rem(self.x + k, 4), self.y, self.z),
            device_id_type=MESH)

    def x_start(self):
        @pl.when(self.holds)
        def _():
            @pl.loop(0, 16)
            def _(k):
                @pl.when(k != self.z)
                def _():
                    block = self.z_in.at[k]
                    pltpu.make_async_remote_copy(
                        src_ref=block, dst_ref=block, send_sem=self.zs.at[0], recv_sem=self.zr.at[k],
                        device_id=device(1 - self.core, self.x, self.y, self.z), device_id_type=MESH).wait_recv()

            sum_rows = self.z_in[0].astype(F32)
            for k in range(1, 16):
                sum_rows = sum_rows + self.z_in[k].astype(F32)
            self.x_out[...] = sum_rows.astype(BF16)

            @pl.loop(1, 8)
            def _(k):
                self.x_copy(k).start()

            self.x_in[self.x] = self.x_out[...]

    def finish(self, out):
        for k in range(3):
            @pl.when(jnp.logical_not(jnp.logical_and(self.holds, self.x == k)))
            def _():
                block = self.x_in.at[k]
                pltpu.make_async_remote_copy(
                    src_ref=block, dst_ref=block, send_sem=self.xs.at[0], recv_sem=self.xr.at[k],
                    device_id=device(1 - self.core, self.x, self.y, self.z), device_id_type=MESH).wait_recv()
            out[:, 384 * k:384 * k + 384] = self.x_in[k, 0:18, :].astype(F32)

    def drain(self):
        self.core_copy().wait_send()
        for upper in range(2):
            for x in range(3):
                pl.when(jnp.logical_not(self.is_me(upper, x)))(
                    lambda: self.plane_copy(upper, x).wait_send())

        @pl.when(self.holds)
        def _():
            @pl.loop(1, 16)
            def _(k):
                self.z_copy(k).wait_send()

            @pl.loop(1, 8)
            def _(k):
                self.x_copy(k).wait_send()


REDUCE_SCRATCH = [
    pltpu.VMEM((2, 288, 1152), BF16),
    pltpu.VMEM((288, 1152), BF16),
    pltpu.VMEM((2, 3, 144, 384), BF16),
    pltpu.VMEM((16, 144, 384), BF16),
    pltpu.VMEM((144, 384), F32),
    pltpu.VMEM((8, 32, 384), BF16),
    pltpu.VMEM((16, 32, 384), BF16),
    pltpu.VMEM((32, 384), BF16),
    pltpu.VMEM((3, 32, 384), BF16),
]
REDUCE_SEMS = [pltpu.SemaphoreType.DMA, pltpu.SemaphoreType.DMA] + [
    pltpu.SemaphoreType.DMA((n,)) for n in (6, 16, 16, 16, 8, 3)]


def reduce_kernel(*refs):
    mixed_t, grad, out = refs[0:3]
    r = Reduce(*refs[3:12], refs[12:20])
    barrier = pltpu.get_barrier_semaphore()
    count = r.greet(barrier)
    for half in range(2):
        r.partial[half] = jnp.dot(
            mixed_t[288 * half:288 * half + 288, :], grad[...], preferred_element_type=F32).astype(BF16)
    pl.semaphore_wait(barrier, count)
    r.core_copy().start()
    r.plane_start()
    r.z_start()
    r.x_start()
    r.finish(out)
    r.drain()


def reduce_grad(mixed_t, grad):
    vmem = pl.BlockSpec(memory_space=pltpu.VMEM)
    return pl.pallas_call(
        reduce_kernel,
        out_shape=jax.ShapeDtypeStruct((18, 1152), F32),
        in_specs=[vmem] * 2,
        out_specs=vmem,
        scratch_shapes=REDUCE_SCRATCH + REDUCE_SEMS,
        compiler_params=pltpu.CompilerParams(
            collective_id=1, has_side_effects=True, vmem_limit_bytes=48 * 2**20),
        name="reduce_grad",
    )(mixed_t, grad)


def split_heads(array):
    return array.reshape(array.shape[:-1] + (HEADS, HEAD))


def join_heads(array):
    return array.reshape(array.shape[:-2] + (HEADS * HEAD,))


def times_transposed(left, right):
    return lax.dot_general(
        left, right, (((1,), (1,)), ((), ())), preferred_element_type=jnp.float32
    )


def attend(queries, key_rows, values, score_scale, visible):
    scores = (
        jnp.einsum("bqhe,bkhe->bhqk", queries, key_rows, preferred_element_type=jnp.float32)
        * score_scale
    )
    if visible is not None:
        scores = jnp.where(visible, scores, -1e30)
    weights = jax.nn.softmax(scores, axis=-1)
    output = jnp.einsum(
        "bhqk,bkhe->bqhe", weights.astype(jnp.bfloat16), values, preferred_element_type=jnp.float32
    )
    return (output.astype(jnp.bfloat16), weights)


def attend_grad(upstream, queries, key_rows, values, weights, score_scale, with_memory):
    prob_grad = jnp.einsum("bqhe,bkhe->bhqk", upstream, values, preferred_element_type=jnp.float32)
    score_grad = (
        weights * (prob_grad - jnp.sum(prob_grad * weights, axis=-1, keepdims=True))
    ).astype(jnp.bfloat16)
    query_grad = (
        score_scale
        * jnp.einsum("bhqk,bkhe->bqhe", score_grad, key_rows, preferred_element_type=jnp.float32)
    ).astype(jnp.bfloat16)
    if not with_memory:
        return query_grad
    value_grad = jnp.einsum(
        "bhqk,bqhe->bkhe",
        weights.astype(jnp.bfloat16),
        upstream,
        preferred_element_type=jnp.float32,
    ).astype(jnp.bfloat16)
    key_grad = (
        score_scale
        * jnp.einsum("bhqk,bqhe->bkhe", score_grad, queries, preferred_element_type=jnp.float32)
    ).astype(jnp.bfloat16)
    return (query_grad, key_grad, value_grad)


def shards(tokens, spatial_qkv, text_kv, text_len, w_os, w_qc, w_oc, w_qkv, cotangent):
    frame_count, patch_count, model_width = (tokens.shape[1], tokens.shape[2], tokens.shape[3])
    inner = HEADS * HEAD
    row_count = frame_count * patch_count
    score_scale = 1.0 / math.sqrt(HEAD)
    full_os, full_qc, full_oc, full_qkv = gather_weights(w_os, w_qc, w_oc, w_qkv)
    spatial = split_heads(spatial_qkv[0])
    spatial_queries, spatial_keys, spatial_values = (
        spatial[:, :, 0],
        spatial[:, :, 1],
        spatial[:, :, 2],
    )
    spatial_out, spatial_weights = attend(
        spatial_queries, spatial_keys, spatial_values, score_scale, None
    )
    mixed = join_heads(spatial_out).reshape(row_count, inner)
    hidden = (
        tokens[0].reshape(row_count, model_width).astype(jnp.float32)
        + jnp.dot(mixed, full_os, preferred_element_type=jnp.float32)
    ).astype(jnp.bfloat16)
    cross_queries = split_heads(
        jnp.dot(hidden, full_qc, preferred_element_type=jnp.float32).astype(jnp.bfloat16)
    )[None]
    text_keys = split_heads(text_kv[0, :, 0])[None]
    text_values = split_heads(text_kv[0, :, 1])[None]
    visible = jnp.arange(text_kv.shape[1]) < text_len[0]
    cross_out, cross_weights = attend(cross_queries, text_keys, text_values, score_scale, visible)
    after = (
        hidden.astype(jnp.float32)
        + jnp.dot(join_heads(cross_out[0]), full_oc, preferred_element_type=jnp.float32)
    ).astype(jnp.bfloat16)
    patched = lax.all_to_all(
        after.reshape(frame_count, patch_count, model_width),
        "seq",
        split_axis=1,
        concat_axis=0,
        tiled=True,
    )
    all_frames, local_patches = (patched.shape[0], patched.shape[1])
    flat_patched = patched.reshape(all_frames * local_patches, model_width)
    projected = jnp.dot(flat_patched, full_qkv, preferred_element_type=jnp.float32)
    temporal = jnp.swapaxes(
        split_heads(projected.astype(jnp.bfloat16).reshape(all_frames, local_patches, 3, inner)),
        0,
        1,
    )
    temporal_queries, temporal_keys, temporal_values = (
        temporal[:, :, 0],
        temporal[:, :, 1],
        temporal[:, :, 2],
    )
    temporal_out, temporal_weights = attend(
        temporal_queries, temporal_keys, temporal_values, score_scale, None
    )
    temporal_heads = jnp.swapaxes(join_heads(temporal_out), 0, 1)[None]
    upstream = split_heads(jnp.swapaxes(cotangent[0], 0, 1))
    temporal_grads = attend_grad(
        upstream,
        temporal_queries,
        temporal_keys,
        temporal_values,
        temporal_weights,
        score_scale,
        True,
    )
    proj_grad = jnp.swapaxes(jnp.stack(temporal_grads, axis=2), 0, 1).reshape(
        all_frames * local_patches, 3 * inner
    )
    patch_grad = times_transposed(proj_grad, full_qkv)
    patch_grad = patch_grad.astype(jnp.bfloat16).reshape(all_frames, local_patches, model_width)
    after_grad = lax.all_to_all(patch_grad, "seq", split_axis=0, concat_axis=1, tiled=True).reshape(
        row_count, model_width
    )
    cross_grad = split_heads(times_transposed(after_grad, full_oc).astype(jnp.bfloat16))[None]
    cross_query_grad = attend_grad(
        cross_grad, cross_queries, text_keys, text_values, cross_weights, score_scale, False
    )
    hidden_grad = (
        after_grad.astype(jnp.float32) + times_transposed(join_heads(cross_query_grad[0]), full_qc)
    ).astype(jnp.bfloat16)
    mixed_grad = times_transposed(hidden_grad, full_os).astype(jnp.bfloat16)
    grad_os = reduce_grad(mixed.T, hidden_grad)
    spatial_grads = attend_grad(
        split_heads(mixed_grad.reshape(frame_count, patch_count, inner)),
        spatial_queries,
        spatial_keys,
        spatial_values,
        spatial_weights,
        score_scale,
        True,
    )
    qkv_grad = join_heads(jnp.stack(spatial_grads, axis=2))[None]
    return (
        temporal_heads,
        hidden_grad.reshape(1, frame_count, patch_count, model_width),
        qkv_grad,
        grad_os,
    )


def solution(mesh):
    placed = (
        P("dp", "seq", None, None),
        P("dp", "seq", None, None, None),
        P("dp", None, None, None),
        P("dp"),
        P("seq", None),
        P("seq", None),
        P("seq", None),
        P("seq", None),
        P("dp", None, "seq", None),
    )
    return jax.shard_map(
        shards,
        mesh=mesh,
        in_specs=placed,
        out_specs=(
            P("dp", None, "seq", None),
            P("dp", "seq", None, None),
            P("dp", "seq", None, None, None),
            P("seq", None),
        ),
        check_vma=False,
    )
```

```python
import math

import jax
import jax.numpy as jnp
from jax import lax
from jax.experimental import pallas as pl
from jax.experimental.pallas import tpu as pltpu
from jax.sharding import PartitionSpec as P

HEADS = 8
HEAD = 72
SCALE = 1.0 / math.sqrt(HEAD)
MESH = pl.DeviceIdType.MESH
BF16 = jnp.bfloat16
F32 = jnp.float32
OS, QC, OC, QKV = range(4)
COLUMNS = (1152, 576, 1152, 1728)
ROWS = (18, 36, 18, 36)
CUTS = {18: (0, 48, 80, 112, 144), 36: (0, 80, 144, 224, 288)}
BLOCKS = ((OS, OC), (QC,), (QKV,))
FAR_CORE = (1, 1, 0)


def place():
    dp, seq = lax.axis_index("dp"), lax.axis_index("seq")
    return lax.rem(dp, 2), lax.div(dp, 4), lax.div(seq, 8), lax.rem(lax.div(dp, 2), 2) * 8 + lax.rem(seq, 8)


def device(core, x, y, z):
    return ((x * 2 + lax.div(z, 8)) * 2 + core, y * 8 + lax.rem(z, 8))


class Gather:
    def __init__(self, shards, landing, full, sems):
        self.shards, self.landing, self.full = shards, landing, full
        (self.zs, self.zr, self.ps, self.pr, self.ws, self.wr, self.qs, self.qr) = sems
        core, x, y, z = place()
        self.core, self.x, self.y, self.slot = core, x, y, lax.rem(z, 8)
        self.step = 1 - 2 * core
        self.next_z = device(core, x, y, lax.rem(z + self.step + 16, 16))
        self.next_y = device(core, x, lax.rem(y + self.step + 4, 4), z)
        self.next_x = device(core, lax.rem(x + self.step + 4, 4), y, z)
        self.partner = device(1 - core, x, y, z)
        self.half = lax.rem(x, 2)

    def stage(self, b):
        block = self.landing[b]
        block[self.slot] = jnp.zeros(block.shape[1:], BF16)
        at = 0
        for w in BLOCKS[b]:
            block[self.slot, at:at + ROWS[w], :] = self.shards[w][...]
            at += ROWS[w]

    def block_copy(self, b, s, slot, to, send, recv):
        block = self.landing[b].at[slot]
        return pltpu.make_async_remote_copy(
            src_ref=block, dst_ref=block, send_sem=send.at[b, s], recv_sem=recv.at[b, s],
            device_id=to, device_id_type=MESH)

    def z_copy(self, b, s, slot):
        return self.block_copy(b, s, slot, self.next_z, self.zs, self.zr)

    def pass_copy(self, b, s, slot):
        return self.block_copy(b, s, slot, self.partner, self.ps, self.pr)

    def away(self, steps):
        return lax.rem(self.slot - steps * self.step + 8, 8)

    def z_start(self, b):
        self.z_copy(b, 0, self.slot).start()

    def z_step(self, b, s):
        def go():
            slot = self.away(s + 1)
            self.z_copy(b, s, slot).wait_recv()
            if s < 2:
                self.z_copy(b, s + 1, slot).start()
            if s == 2:
                pl.when(self.core == FAR_CORE[b])(lambda: self.z_copy(b, 3, slot).start())
            self.pass_copy(b, s, slot).start()

        if s < 3:
            go()
        else:
            pl.when(self.core == FAR_CORE[b])(go)

    def z_finish(self, b):
        for s in range(3):
            self.pass_copy(b, s, lax.rem(self.slot + (s + 1) * self.step + 8, 8)).wait_recv()
        pl.when(self.core != FAR_CORE[b])(
            lambda: self.pass_copy(b, 3, lax.rem(self.slot + 4, 8)).wait_recv())

    def pack(self, w):
        b = [k for k in range(3) if w in BLOCKS[k]][0]
        at, rows = ROWS[w] * BLOCKS[b].index(w), ROWS[w]
        for k in range(8):
            self.full[w][self.y, k * rows:(k + 1) * rows, :] = self.landing[b][k, at:at + rows, :]
        self.by_half(w, self.half, lambda c: c(self.y, None, self.next_y, 0, self.ws, self.wr).start())

    def part_copy(self, w, half, share, quarter, to, s, send, recv):
        cuts = CUTS[ROWS[w]]
        first, last = (cuts[2 * half], cuts[2 * half + 2]) if share is None else (
            cuts[2 * half + share], cuts[2 * half + share + 1])
        block = self.full[w].at[quarter, pl.ds(first, last - first)]
        return pltpu.make_async_remote_copy(
            src_ref=block, dst_ref=block, send_sem=send.at[w, s], recv_sem=recv.at[w, s],
            device_id=to, device_id_type=MESH)

    def by_half(self, w, half, go):
        for h in range(2):
            @pl.when(half == h)
            def _():
                go(lambda quarter, share, to, s, send, recv: self.part_copy(
                    w, h, share, quarter, to, s, send, recv))

    def by_share(self, w, half, share, go):
        for c in range(2):
            @pl.when(share == c)
            def _():
                self.by_half(w, half, lambda copy: go(lambda quarter, to, s, send, recv: copy(
                    quarter, c, to, s, send, recv)))

    def near(self):
        return lax.rem(self.y - self.step + 4, 4)

    def far(self):
        return lax.rem(self.y + 2, 4)

    def y_step(self, w):
        def near(copy):
            copy(self.near(), None, self.next_y, 0, self.ws, self.wr).wait_recv()
            copy(self.near(), None, self.next_x, 2, self.ws, self.wr).start()
            copy(self.near(), None, self.partner, 0, self.qs, self.qr).start()

        self.by_half(w, self.half, near)
        self.by_share(w, self.half, self.core, lambda copy: copy(
            self.near(), self.next_y, 1, self.ws, self.wr).start())

    def y_last(self, w):
        def far(copy):
            copy(self.far(), self.next_y, 1, self.ws, self.wr).wait_recv()
            copy(self.far(), self.next_x, 3, self.ws, self.wr).start()
            copy(self.far(), self.partner, 1, self.qs, self.qr).start()

        self.by_share(w, self.half, self.core, far)

    def x_step(self, w):
        def near(copy):
            copy(self.near(), None, self.next_x, 2, self.ws, self.wr).wait_recv()
            copy(self.near(), None, self.partner, 2, self.qs, self.qr).start()

        self.by_half(w, 1 - self.half, near)

    def x_last(self, w):
        def far(copy):
            copy(self.far(), self.next_x, 3, self.ws, self.wr).wait_recv()
            copy(self.far(), self.partner, 3, self.qs, self.qr).start()

        self.by_share(w, 1 - self.half, self.core, far)

    def finish(self, w):
        other = lax.rem(self.y + self.step + 4, 4)
        self.by_half(w, self.half, lambda copy: copy(
            other, None, self.partner, 0, self.qs, self.qr).wait_recv())
        self.by_half(w, 1 - self.half, lambda copy: copy(
            other, None, self.partner, 2, self.qs, self.qr).wait_recv())
        self.by_share(w, self.half, 1 - self.core, lambda copy: copy(
            self.far(), self.partner, 1, self.qs, self.qr).wait_recv())
        self.by_share(w, 1 - self.half, 1 - self.core, lambda copy: copy(
            self.far(), self.partner, 3, self.qs, self.qr).wait_recv())

    def drain(self):
        for b in range(3):
            for s in range(3):
                self.z_copy(b, s, self.away(s)).wait_send()
                self.pass_copy(b, s, self.away(s + 1)).wait_send()

            @pl.when(self.core == FAR_CORE[b])
            def _():
                self.z_copy(b, 3, self.away(3)).wait_send()
                self.pass_copy(b, 3, self.away(4)).wait_send()

        for w in range(4):
            def mine(copy):
                copy(self.y, None, self.next_y, 0, self.ws, self.wr).wait_send()
                copy(self.near(), None, self.next_x, 2, self.ws, self.wr).wait_send()
                copy(self.near(), None, self.partner, 0, self.qs, self.qr).wait_send()

            def mine_far(copy):
                copy(self.near(), self.next_y, 1, self.ws, self.wr).wait_send()
                copy(self.far(), self.next_x, 3, self.ws, self.wr).wait_send()
                copy(self.far(), self.partner, 1, self.qs, self.qr).wait_send()

            self.by_half(w, self.half, mine)
            self.by_half(w, 1 - self.half, lambda copy: copy(
                self.near(), None, self.partner, 2, self.qs, self.qr).wait_send())
            self.by_share(w, self.half, self.core, mine_far)
            self.by_share(w, 1 - self.half, self.core, lambda copy: copy(
                self.far(), self.partner, 3, self.qs, self.qr).wait_send())


class Switch:
    def __init__(self, out, taken, send, recv):
        self.out, self.taken, self.send, self.recv = out, taken, send, recv
        self.dp, self.seq = lax.axis_index("dp"), lax.axis_index("seq")

    def copy(self, k):
        to = lax.rem(self.seq + k, 32)
        return pltpu.make_async_remote_copy(
            src_ref=self.out.at[to], dst_ref=self.taken.at[self.seq],
            send_sem=self.send.at[k], recv_sem=self.recv.at[k],
            device_id=(self.dp, to), device_id_type=MESH)

    def start(self):
        @pl.loop(1, 32)
        def _(k):
            self.copy(k).start()

        self.taken[self.seq] = self.out[self.seq]

    def wait(self):
        @pl.loop(1, 32)
        def _(k):
            block = self.taken.at[lax.rem(self.seq - k + 32, 32)]
            pltpu.make_async_remote_copy(
                src_ref=block, dst_ref=block, send_sem=self.send.at[k], recv_sem=self.recv.at[k],
                device_id=(self.dp, lax.rem(self.seq + k, 32)), device_id_type=MESH).wait_recv()

    def drain(self):
        @pl.loop(1, 32)
        def _(k):
            self.copy(k).wait_send()


class Reduce:
    def __init__(self, partial, taken, pieces, plane, total, z_out, z_in, x_out, x_in, sems):
        self.partial, self.taken, self.pieces, self.plane = partial, taken, pieces, plane
        self.total, self.z_out, self.z_in, self.x_out, self.x_in = total, z_out, z_in, x_out, x_in
        (self.cs, self.cr, self.ps, self.pr, self.zs, self.zr, self.xs, self.xr) = sems
        self.core, self.x, self.y, self.z = place()
        self.holds = jnp.logical_and(self.x < 3, lax.div(self.y, 2) == self.core)
        self.me = self.x * 4 + self.y

    def greet(self, barrier):
        def signal(d):
            pl.semaphore_signal(barrier, inc=1, device_id=d, device_id_type=MESH)

        core, x, y, z = self.core, self.x, self.y, self.z

        @pl.loop(1, 16)
        def _(k):
            signal(device(core, lax.rem(x + lax.div(k, 4), 4), lax.rem(y + lax.rem(k, 4), 4), z))
            signal(device(core, x, y, lax.rem(z + k, 16)))

        @pl.loop(0, 4)
        def _(k):
            signal(device(1 - core, lax.rem(x + k, 4), y, z))

        return 34

    def core_copy(self):
        return pltpu.make_async_remote_copy(
            src_ref=self.partial.at[1 - self.core], dst_ref=self.taken, send_sem=self.cs, recv_sem=self.cr,
            device_id=device(1 - self.core, self.x, self.y, self.z), device_id_type=MESH)

    def plane_copy(self, upper, x):
        return pltpu.make_async_remote_copy(
            src_ref=self.pieces.at[upper, x], dst_ref=self.plane.at[self.me],
            send_sem=self.ps.at[upper * 3 + x], recv_sem=self.pr.at[self.me],
            device_id=device(self.core, x, self.core * 2 + upper, self.z), device_id_type=MESH)

    def is_me(self, upper, x):
        return jnp.logical_and(self.x == x, self.y == self.core * 2 + upper)

    def plane_start(self):
        self.core_copy().wait_recv()
        for upper in range(2):
            for x in range(3):
                rows, columns = slice(144 * upper, 144 * upper + 144), slice(384 * x, 384 * x + 384)
                self.pieces[upper, x] = (
                    self.partial[self.core, rows, columns].astype(F32)
                    + self.taken[rows, columns].astype(F32)).astype(BF16)
        for upper in range(2):
            for x in range(3):
                pl.when(jnp.logical_not(self.is_me(upper, x)))(
                    lambda: self.plane_copy(upper, x).start())

                @pl.when(self.is_me(upper, x))
                def _():
                    self.plane[self.me] = self.pieces[upper, x]

    def z_copy(self, k):
        to = lax.rem(self.z + k, 16)
        return pltpu.make_async_remote_copy(
            src_ref=self.z_out.at[lax.rem(to, 8)], dst_ref=self.z_in.at[self.z],
            send_sem=self.zs.at[k], recv_sem=self.zr.at[self.z],
            device_id=device(self.core, self.x, self.y, to), device_id_type=MESH)

    def z_start(self):
        @pl.when(self.holds)
        def _():
            @pl.loop(0, 16)
            def _(k):
                @pl.when(k != self.me)
                def _():
                    block = self.plane.at[k]
                    pltpu.make_async_remote_copy(
                        src_ref=block, dst_ref=block, send_sem=self.ps.at[0], recv_sem=self.pr.at[k],
                        device_id=device(1 - self.core, self.x, self.y, self.z), device_id_type=MESH).wait_recv()

            for r in range(3):
                rows = slice(48 * r, 48 * r + 48)
                sum_rows = self.plane[0, rows].astype(F32)
                for k in range(1, 16):
                    sum_rows = sum_rows + self.plane[k, rows].astype(F32)
                self.total[rows] = sum_rows
            self.z_out[...] = jnp.zeros(self.z_out.shape, BF16)
            for k in range(8):
                self.z_out[k, 0:18, :] = self.total[18 * k:18 * k + 18, :].astype(BF16)

            @pl.loop(1, 16)
            def _(k):
                self.z_copy(k).start()

            self.z_in[self.z] = self.z_out[lax.rem(self.z, 8)]

    def x_copy(self, k):
        other = lax.div(k, 4)
        return pltpu.make_async_remote_copy(
            src_ref=self.x_out, dst_ref=self.x_in.at[self.x],
            send_sem=self.xs.at[k], recv_sem=self.xr.at[self.x],
            device_id=device(lax.rem(self.core + other, 2), lax.rem(self.x + k, 4), self.y, self.z),
            device_id_type=MESH)

    def x_start(self):
        @pl.when(self.holds)
        def _():
            @pl.loop(0, 16)
            def _(k):
                @pl.when(k != self.z)
                def _():
                    block = self.z_in.at[k]
                    pltpu.make_async_remote_copy(
                        src_ref=block, dst_ref=block, send_sem=self.zs.at[0], recv_sem=self.zr.at[k],
                        device_id=device(1 - self.core, self.x, self.y, self.z), device_id_type=MESH).wait_recv()

            sum_rows = self.z_in[0].astype(F32)
            for k in range(1, 16):
                sum_rows = sum_rows + self.z_in[k].astype(F32)
            self.x_out[...] = sum_rows.astype(BF16)

            @pl.loop(1, 8)
            def _(k):
                self.x_copy(k).start()

            self.x_in[self.x] = self.x_out[...]

    def finish(self, out):
        for k in range(3):
            @pl.when(jnp.logical_not(jnp.logical_and(self.holds, self.x == k)))
            def _():
                block = self.x_in.at[k]
                pltpu.make_async_remote_copy(
                    src_ref=block, dst_ref=block, send_sem=self.xs.at[0], recv_sem=self.xr.at[k],
                    device_id=device(1 - self.core, self.x, self.y, self.z), device_id_type=MESH).wait_recv()
            out[:, 384 * k:384 * k + 384] = self.x_in[k, 0:18, :].astype(F32)

    def drain(self):
        self.core_copy().wait_send()
        for upper in range(2):
            for x in range(3):
                pl.when(jnp.logical_not(self.is_me(upper, x)))(
                    lambda: self.plane_copy(upper, x).wait_send())

        @pl.when(self.holds)
        def _():
            @pl.loop(1, 16)
            def _(k):
                self.z_copy(k).wait_send()

            @pl.loop(1, 8)
            def _(k):
                self.x_copy(k).wait_send()


REDUCE_SCRATCH = [
    pltpu.VMEM((2, 288, 1152), BF16),
    pltpu.VMEM((288, 1152), BF16),
    pltpu.VMEM((2, 3, 144, 384), BF16),
    pltpu.VMEM((16, 144, 384), BF16),
    pltpu.VMEM((144, 384), F32),
    pltpu.VMEM((8, 32, 384), BF16),
    pltpu.VMEM((16, 32, 384), BF16),
    pltpu.VMEM((32, 384), BF16),
    pltpu.VMEM((3, 32, 384), BF16),
]
REDUCE_SEMS = [pltpu.SemaphoreType.DMA, pltpu.SemaphoreType.DMA] + [
    pltpu.SemaphoreType.DMA((n,)) for n in (6, 16, 16, 16, 8, 3)]


def times(left, right):
    return jnp.dot(left, right, preferred_element_type=F32)


def times_transposed(left, right):
    return lax.dot_general(left, right, (((1,), (1,)), ((), ())), preferred_element_type=F32)


def transposed_times(left, right):
    return lax.dot_general(left, right, (((0,), (0,)), ((), ())), preferred_element_type=F32)


def split_heads(ref, array):
    for h in range(HEADS):
        ref[h] = array[HEAD * h:HEAD * h + HEAD, :]


def attend(head, queries, keys, values, visible, weights, out):
    scores = transposed_times(keys[head], queries[head]) * SCALE
    if visible is not None:
        scores = jnp.where(visible, scores, -1e30)
    powers = jnp.exp(scores - jnp.max(scores, axis=0, keepdims=True))
    share = powers / jnp.sum(powers, axis=0, keepdims=True)
    weights[head] = share
    out[head] = times(values[head], share.astype(BF16)).astype(BF16)


def attend_grad(head, upstream, queries, keys, values, weights, query_grad, key_grad, value_grad):
    upper, share = upstream[head], weights[head]
    share_grad = transposed_times(values[head], upper)
    score_grad = (share * (share_grad - jnp.sum(share_grad * share, axis=0, keepdims=True))).astype(BF16)
    query_grad[head] = (SCALE * times(keys[head], score_grad)).astype(BF16)
    if key_grad is not None:
        value_grad[head] = times_transposed(upper, share.astype(BF16)).astype(BF16)
        key_grad[head] = (SCALE * times_transposed(queries[head], score_grad)).astype(BF16)


def each_head(go):
    @pl.loop(0, HEADS // 2)
    def _(pair):
        go(2 * pair)
        go(2 * pair + 1)


def block_pair(
    tokens, qkv, text, length, w_os, w_qc, w_oc, w_qkv, cotangent,
    heads_out, tokens_grad, qkv_grad, os_grad,
    full_os, full_qc, full_oc, full_qkv, land_pair, land_qc, land_qkv,
    gz_send, gz_recv, gp_send, gp_recv, gw_send, gw_recv, gq_send, gq_recv,
    to_patches, from_frames, to_frames, from_patches, s1_send, s1_recv, s2_send, s2_recv,
    spatial_w, cross_w, temporal_w, mixed_heads, mixed_t, cross_queries, cross_heads, temporal, upstream,
    temporal_heads, temporal_grads, wide_t, hidden_ref, *reduce_refs,
):
    full = (full_os, full_qc, full_oc, full_qkv)
    g = Gather((w_os, w_qc, w_oc, w_qkv), (land_pair, land_qc, land_qkv), full,
               (gz_send, gz_recv, gp_send, gp_recv, gw_send, gw_recv, gq_send, gq_recv))
    forth = Switch(to_patches, from_frames, s1_send, s1_recv)
    back = Switch(to_frames, from_patches, s2_send, s2_recv)
    r = Reduce(*reduce_refs[0:9], reduce_refs[9:17])

    barrier = pltpu.get_barrier_semaphore()
    greeted = r.greet(barrier)
    core, x, y, z = place()

    @pl.loop(0, 21)
    def _(k):
        to = device(core, x, lax.rem(y + 1 + lax.div(k, 7), 4),
                    lax.div(z, 8) * 8 + lax.rem(z + 1 + lax.rem(k, 7), 8))
        pl.semaphore_signal(barrier, inc=1, device_id=to, device_id_type=MESH)

    for b in range(3):
        g.stage(b)
    pl.semaphore_wait(barrier, greeted + 21)

    def whole(w):
        return full[w][...].reshape(-1, COLUMNS[w])

    def join(heads, groups=1):
        for i in range(groups):
            for h in range(HEADS):
                at = (i * HEADS + h) * HEAD
                wide_t[at:at + HEAD, :] = heads[i, h] if groups > 1 else heads[h]
        return wide_t[0:groups * HEADS * HEAD, :].T

    g.z_start(0)
    g.z_start(1)
    for s in range(4):
        for h in (2 * s, 2 * s + 1):
            attend(h, qkv.at[0], qkv.at[1], qkv.at[2], None, spatial_w, mixed_heads)
        g.z_step(0, s)
        g.z_step(1, s)
    g.z_start(2)
    g.z_finish(0)
    g.pack(OS)
    g.z_finish(1)
    g.pack(QC)
    g.pack(OC)
    mixed = join(mixed_heads)
    mixed_t[...] = wide_t[0:576, :]
    g.z_step(2, 0)
    g.y_step(OS)
    g.y_step(QC)
    g.y_last(OS)
    g.z_step(2, 1)
    g.x_step(OS)
    g.y_step(OC)
    g.y_last(QC)
    g.x_last(OS)
    g.x_step(QC)
    g.z_step(2, 2)
    g.finish(OS)
    hidden = (tokens[...].astype(F32) + times(mixed, whole(OS))).astype(BF16)
    hidden_ref[...] = hidden
    g.y_last(OC)
    g.x_step(OC)
    g.x_last(QC)
    g.z_step(2, 3)
    g.finish(QC)
    split_heads(cross_queries, times(hidden, whole(QC)).astype(BF16).T)
    g.x_last(OC)
    g.z_finish(2)
    g.pack(QKV)
    seen = lax.broadcasted_iota(jnp.int32, (128, 128), 0) < length[0]
    each_head(lambda h: attend(h, cross_queries, text.at[0], text.at[1], seen, cross_w, cross_heads))
    g.finish(OC)
    after = (hidden_ref[...].astype(F32) + times(join(cross_heads), whole(OC))).astype(BF16)
    to_patches[...] = after.reshape(32, 4, 1152)
    forth.start()
    g.y_step(QKV)
    split_heads(upstream, cotangent[...].reshape(128, 576).T)
    g.y_last(QKV)
    g.x_step(QKV)
    g.x_last(QKV)
    g.finish(QKV)
    forth.wait()

    projected = times(from_frames[...].reshape(128, 1152), whole(QKV)).astype(BF16).T
    for i in range(3):
        split_heads(temporal.at[i], projected[576 * i:576 * i + 576, :])
    same = (lax.rem(lax.broadcasted_iota(jnp.int32, (128, 128), 0), 4)
            == lax.rem(lax.broadcasted_iota(jnp.int32, (128, 128), 1), 4))

    def temporal_head(h):
        attend(h, temporal.at[0], temporal.at[1], temporal.at[2], same, temporal_w, temporal_heads)
        attend_grad(h, upstream, temporal.at[0], temporal.at[1], temporal.at[2], temporal_w,
                    temporal_grads.at[0], temporal_grads.at[1], temporal_grads.at[2])

    each_head(temporal_head)
    patch_grad = times_transposed(join(temporal_grads, 3), whole(QKV)).astype(BF16)
    to_frames[...] = patch_grad.reshape(32, 4, 1152)
    back.start()
    heads_out[...] = join(temporal_heads).reshape(32, 4, 576)
    g.drain()
    forth.drain()
    back.wait()

    after_grad = from_patches[...].reshape(128, 1152)
    split_heads(upstream, times_transposed(after_grad, whole(OC)).astype(BF16).T)
    each_head(lambda h: attend_grad(
        h, upstream, cross_queries, text.at[0], text.at[1], cross_w, cross_heads, None, None))
    hidden_grad = (after_grad.astype(F32) + times_transposed(join(cross_heads), whole(QC))).astype(BF16)
    tokens_grad[...] = hidden_grad
    for half in range(2):
        r.partial[half] = times(mixed_t[288 * half:288 * half + 288, :], hidden_grad).astype(BF16)
    r.core_copy().start()
    split_heads(upstream, times_transposed(hidden_grad, whole(OS)).astype(BF16).T)
    r.plane_start()
    each_head(lambda h: attend_grad(
        h, upstream, qkv.at[0], qkv.at[1], qkv.at[2], spatial_w, qkv_grad.at[0], qkv_grad.at[1],
        qkv_grad.at[2]))
    r.z_start()
    r.x_start()
    r.finish(os_grad)
    back.drain()
    r.drain()


def shards(tokens, spatial_qkv, text_kv, text_len, w_os, w_qc, w_oc, w_qkv, cotangent):
    heads = (HEADS, HEAD, 128)
    vmem = pl.BlockSpec(memory_space=pltpu.VMEM)
    dma = pltpu.SemaphoreType.DMA
    slabs = pltpu.VMEM((32, 4, 1152), BF16)
    temporal_heads, tokens_grad, qkv_grad, os_grad = pl.pallas_call(
        block_pair,
        out_shape=[
            jax.ShapeDtypeStruct((32, 4, 576), BF16),
            jax.ShapeDtypeStruct((128, 1152), BF16),
            jax.ShapeDtypeStruct((3,) + heads, BF16),
            jax.ShapeDtypeStruct((18, 1152), F32),
        ],
        in_specs=[vmem] * 3 + [pl.BlockSpec(memory_space=pltpu.SMEM)] + [vmem] * 5,
        out_specs=[vmem] * 4,
        scratch_shapes=[pltpu.VMEM((4, 8 * rows, columns), BF16) for rows, columns in zip(ROWS, COLUMNS)]
        + [pltpu.VMEM((8, 48, columns), BF16) for columns in (1152, 576, 1728)]
        + [dma((3, 4))] * 4 + [dma((4, 4))] * 4
        + [slabs] * 4 + [dma((32,))] * 4
        + [pltpu.VMEM((HEADS, 128, 128), F32)] * 3
        + [pltpu.VMEM(heads, BF16), pltpu.VMEM((576, 128), BF16), pltpu.VMEM(heads, BF16), pltpu.VMEM(heads, BF16),
           pltpu.VMEM((3,) + heads, BF16), pltpu.VMEM(heads, BF16), pltpu.VMEM(heads, BF16),
           pltpu.VMEM((3,) + heads, BF16), pltpu.VMEM((1728, 128), BF16), pltpu.VMEM((128, 1152), BF16)]
        + REDUCE_SCRATCH + REDUCE_SEMS,
        compiler_params=pltpu.CompilerParams(
            collective_id=0, has_side_effects=True, vmem_limit_bytes=56 * 2**20),
        name="block_pair",
    )(
        tokens.reshape(128, 1152),
        jnp.transpose(spatial_qkv[0, 0], (1, 2, 0)).reshape((3,) + heads),
        jnp.transpose(text_kv[0], (1, 2, 0)).reshape((2,) + heads),
        text_len, w_os, w_qc, w_oc, w_qkv,
        cotangent.reshape(32, 4, 576),
    )
    return (
        temporal_heads[None],
        tokens_grad[None, None],
        jnp.transpose(qkv_grad.reshape(3, 576, 128), (2, 0, 1))[None, None],
        os_grad,
    )


def solution(mesh):
    placed = (
        P("dp", "seq", None, None),
        P("dp", "seq", None, None, None),
        P("dp", None, None, None),
        P("dp"),
        P("seq", None),
        P("seq", None),
        P("seq", None),
        P("seq", None),
        P("dp", None, "seq", None),
    )
    return jax.shard_map(
        shards,
        mesh=mesh,
        in_specs=placed,
        out_specs=(
            P("dp", None, "seq", None),
            P("dp", "seq", None, None),
            P("dp", "seq", None, None, None),
            P("seq", None),
        ),
        check_vma=False,
    )
```

```python
import math

import jax
import jax.numpy as jnp
from jax import lax
from jax.experimental import pallas as pl
from jax.experimental.pallas import tpu as pltpu
from jax.sharding import PartitionSpec as P

HEADS = 8
HEAD = 72
SCALE = 1.0 / math.sqrt(HEAD)
MESH = pl.DeviceIdType.MESH
BF16 = jnp.bfloat16
F32 = jnp.float32
OS, QC, OC, TQ, TK, TV = WEIGHTS = range(6)
COLUMNS = (1152, 576, 1152, 576, 576, 576)
ROWS = (18, 36, 18, 36, 36, 36)
CUTS = {18: (0, 48, 80, 112, 144), 36: (0, 80, 144, 224, 288)}
FAR_CORE = (1, 1, 1, 0, 0, 0)


def place():
    dp, seq = lax.axis_index("dp"), lax.axis_index("seq")
    return lax.rem(dp, 2), lax.div(dp, 4), lax.div(seq, 8), lax.rem(lax.div(dp, 2), 2) * 8 + lax.rem(seq, 8)


def device(core, x, y, z):
    return ((x * 2 + lax.div(z, 8)) * 2 + core, y * 8 + lax.rem(z, 8))


def greet(barrier):
    core, x, y, z = place()

    def signal(*to):
        pl.semaphore_signal(barrier, inc=1, device_id=device(*to), device_id_type=MESH)

    @pl.loop(1, 16)
    def _(k):
        signal(core, x, y, lax.rem(z + k, 16))

    @pl.loop(0, 4)
    def _(k):
        signal(1 - core, lax.rem(x + k, 4), y, z)

    for k in range(1, 4):
        side = lax.rem(y + k, 4)

        @pl.loop(0, 8)
        def _(j):
            signal(core, x, side, lax.div(z, 8) * 8 + j)

        for j in range(4):
            if j:
                signal(core, lax.rem(x + j, 4), side, z)
        signal(core, lax.rem(x + k, 4), y, z)
    return 55


class Gather:
    def __init__(self, shards, landing, full, sems):
        self.shards, self.landing, self.full = shards, landing, full
        (self.zs, self.zr, self.ps, self.pr, self.ws, self.wr, self.qs, self.qr) = sems
        core, x, y, z = place()
        self.core, self.x, self.y, self.slot = core, x, y, lax.rem(z, 8)
        self.step = 1 - 2 * core
        self.next_z = device(core, x, y, lax.rem(z + self.step + 16, 16))
        self.next_y = device(core, x, lax.rem(y + self.step + 4, 4), z)
        self.next_x = device(core, lax.rem(x + self.step + 4, 4), y, z)
        self.partner = device(1 - core, x, y, z)
        self.half = lax.rem(x, 2)

    def stage(self, b):
        shard = self.shards[min(b, TQ)]
        first = 576 * max(b - TQ, 0)
        self.landing[b][self.slot] = shard[:, first:first + COLUMNS[b]]

    def block_copy(self, b, s, slot, to, send, recv):
        block = self.landing[b].at[slot]
        return pltpu.make_async_remote_copy(
            src_ref=block, dst_ref=block, send_sem=send.at[b, s], recv_sem=recv.at[b, s],
            device_id=to, device_id_type=MESH)

    def z_copy(self, b, s, slot):
        return self.block_copy(b, s, slot, self.next_z, self.zs, self.zr)

    def pass_copy(self, b, s, slot):
        return self.block_copy(b, s, slot, self.partner, self.ps, self.pr)

    def away(self, steps):
        return lax.rem(self.slot - steps * self.step + 8, 8)

    def z_start(self, b):
        self.z_copy(b, 0, self.slot).start()

    def z_step(self, b, s):
        def go():
            slot = self.away(s + 1)
            self.z_copy(b, s, slot).wait_recv()
            if s < 2:
                self.z_copy(b, s + 1, slot).start()
            if s == 2:
                pl.when(self.core == FAR_CORE[b])(lambda: self.z_copy(b, 3, slot).start())
            self.pass_copy(b, s, slot).start()

        if s < 3:
            go()
        else:
            pl.when(self.core == FAR_CORE[b])(go)

    def z_finish(self, b):
        for s in range(3):
            self.pass_copy(b, s, lax.rem(self.slot + (s + 1) * self.step + 8, 8)).wait_recv()
        pl.when(self.core != FAR_CORE[b])(
            lambda: self.pass_copy(b, 3, lax.rem(self.slot + 4, 8)).wait_recv())

    def pack(self, w):
        rows = ROWS[w]
        for k in range(8):
            self.full[w][self.y, k * rows:(k + 1) * rows, :] = self.landing[w][k]
        self.by_half(w, self.half, lambda c: c(self.y, None, self.next_y, 0, self.ws, self.wr).start())

    def part_copy(self, w, half, share, quarter, to, s, send, recv):
        cuts = CUTS[ROWS[w]]
        first, last = (cuts[2 * half], cuts[2 * half + 2]) if share is None else (
            cuts[2 * half + share], cuts[2 * half + share + 1])
        block = self.full[w].at[quarter, pl.ds(first, last - first)]
        return pltpu.make_async_remote_copy(
            src_ref=block, dst_ref=block, send_sem=send.at[w, s], recv_sem=recv.at[w, s],
            device_id=to, device_id_type=MESH)

    def by_half(self, w, half, go):
        for h in range(2):
            @pl.when(half == h)
            def _():
                go(lambda quarter, share, to, s, send, recv: self.part_copy(
                    w, h, share, quarter, to, s, send, recv))

    def by_share(self, w, half, share, go):
        for c in range(2):
            @pl.when(share == c)
            def _():
                self.by_half(w, half, lambda copy: go(lambda quarter, to, s, send, recv: copy(
                    quarter, c, to, s, send, recv)))

    def near(self):
        return lax.rem(self.y - self.step + 4, 4)

    def far(self):
        return lax.rem(self.y + 2, 4)

    def y_step(self, w):
        def near(copy):
            copy(self.near(), None, self.next_y, 0, self.ws, self.wr).wait_recv()
            copy(self.near(), None, self.next_x, 2, self.ws, self.wr).start()
            copy(self.near(), None, self.partner, 0, self.qs, self.qr).start()

        self.by_half(w, self.half, near)
        self.by_share(w, self.half, self.core, lambda copy: copy(
            self.near(), self.next_y, 1, self.ws, self.wr).start())

    def y_last(self, w):
        def far(copy):
            copy(self.far(), self.next_y, 1, self.ws, self.wr).wait_recv()
            copy(self.far(), self.next_x, 3, self.ws, self.wr).start()
            copy(self.far(), self.partner, 1, self.qs, self.qr).start()

        self.by_share(w, self.half, self.core, far)

    def x_step(self, w):
        def near(copy):
            copy(self.near(), None, self.next_x, 2, self.ws, self.wr).wait_recv()
            copy(self.near(), None, self.partner, 2, self.qs, self.qr).start()

        self.by_half(w, 1 - self.half, near)

    def x_last(self, w):
        def far(copy):
            copy(self.far(), self.next_x, 3, self.ws, self.wr).wait_recv()
            copy(self.far(), self.partner, 3, self.qs, self.qr).start()

        self.by_share(w, 1 - self.half, self.core, far)

    def finish(self, w):
        other = lax.rem(self.y + self.step + 4, 4)
        self.by_half(w, self.half, lambda copy: copy(
            other, None, self.partner, 0, self.qs, self.qr).wait_recv())
        self.by_half(w, 1 - self.half, lambda copy: copy(
            other, None, self.partner, 2, self.qs, self.qr).wait_recv())
        self.by_share(w, self.half, 1 - self.core, lambda copy: copy(
            self.far(), self.partner, 1, self.qs, self.qr).wait_recv())
        self.by_share(w, 1 - self.half, 1 - self.core, lambda copy: copy(
            self.far(), self.partner, 3, self.qs, self.qr).wait_recv())

    def drain(self):
        for b in WEIGHTS:
            for s in range(3):
                self.z_copy(b, s, self.away(s)).wait_send()
                self.pass_copy(b, s, self.away(s + 1)).wait_send()

            @pl.when(self.core == FAR_CORE[b])
            def _():
                self.z_copy(b, 3, self.away(3)).wait_send()
                self.pass_copy(b, 3, self.away(4)).wait_send()

        for w in WEIGHTS:
            def mine(copy):
                copy(self.y, None, self.next_y, 0, self.ws, self.wr).wait_send()
                copy(self.near(), None, self.next_x, 2, self.ws, self.wr).wait_send()
                copy(self.near(), None, self.partner, 0, self.qs, self.qr).wait_send()

            def mine_far(copy):
                copy(self.near(), self.next_y, 1, self.ws, self.wr).wait_send()
                copy(self.far(), self.next_x, 3, self.ws, self.wr).wait_send()
                copy(self.far(), self.partner, 1, self.qs, self.qr).wait_send()

            self.by_half(w, self.half, mine)
            self.by_half(w, 1 - self.half, lambda copy: copy(
                self.near(), None, self.partner, 2, self.qs, self.qr).wait_send())
            self.by_share(w, self.half, self.core, mine_far)
            self.by_share(w, 1 - self.half, self.core, lambda copy: copy(
                self.far(), self.partner, 3, self.qs, self.qr).wait_send())


class Switch:
    def __init__(self, out, taken, send, recv):
        self.out, self.taken, self.send, self.recv = out, taken, send, recv
        self.dp, self.seq = lax.axis_index("dp"), lax.axis_index("seq")

    def copy(self, half, k):
        to = lax.rem(self.seq + k, 32)
        return pltpu.make_async_remote_copy(
            src_ref=self.out.at[half, to], dst_ref=self.taken.at[half, self.seq],
            send_sem=self.send.at[half, k], recv_sem=self.recv.at[half, k],
            device_id=(self.dp, to), device_id_type=MESH)

    def start(self, half):
        @pl.loop(1, 32)
        def _(k):
            self.copy(half, k).start()

        self.taken[half, self.seq] = self.out[half, self.seq]

    def wait(self, half):
        @pl.loop(1, 32)
        def _(k):
            block = self.taken.at[half, lax.rem(self.seq - k + 32, 32)]
            pltpu.make_async_remote_copy(
                src_ref=block, dst_ref=block, send_sem=self.send.at[half, k], recv_sem=self.recv.at[half, k],
                device_id=(self.dp, lax.rem(self.seq + k, 32)), device_id_type=MESH).wait_recv()

    def drain(self):
        for half in range(2):
            @pl.loop(1, 32)
            def _(k):
                self.copy(half, k).wait_send()


class Reduce:
    def __init__(self, theirs, ours, taken, pieces, plane, total, z_out, z_in, x_out, x_in, sems):
        self.theirs, self.ours, self.taken, self.pieces, self.plane = theirs, ours, taken, pieces, plane
        self.total, self.z_out, self.z_in, self.x_out, self.x_in = total, z_out, z_in, x_out, x_in
        (self.cs, self.cr, self.ps, self.pr, self.zs, self.zr, self.xs, self.xr) = sems
        self.core, self.x, self.y, self.z = place()
        self.holds = jnp.logical_and(self.x < 3, lax.div(self.y, 2) == self.core)
        self.me = self.x * 4 + self.y

    def core_copy(self, part):
        return pltpu.make_async_remote_copy(
            src_ref=self.theirs.at[part], dst_ref=self.taken.at[part],
            send_sem=self.cs.at[part], recv_sem=self.cr.at[part],
            device_id=device(1 - self.core, self.x, self.y, self.z), device_id_type=MESH)

    def core_start(self, mixed_t, grad):
        half = times(mixed_t[1 - self.core], grad)
        for part in range(2):
            for upper in range(2):
                at = 144 * upper + 72 * part
                self.theirs[part, upper] = half[at:at + 72].astype(BF16)
            self.core_copy(part).start()
        half = times(mixed_t[self.core], grad)
        for part in range(2):
            for upper in range(2):
                at = 144 * upper + 72 * part
                self.ours[part, upper] = half[at:at + 72]

    def plane_copy(self, part, k):
        piece = lax.rem(k + self.x + 2 * self.y, 6)
        upper, x = lax.div(piece, 3), lax.rem(piece, 3)
        mine = jnp.logical_and(self.x == x, self.y == self.core * 2 + upper)
        copy = pltpu.make_async_remote_copy(
            src_ref=self.pieces.at[part, upper, x], dst_ref=self.plane.at[part, self.me],
            send_sem=self.ps.at[part, k], recv_sem=self.pr.at[part, self.me],
            device_id=device(self.core, x, self.core * 2 + upper, self.z), device_id_type=MESH)
        return mine, copy

    def plane_start(self, part):
        self.core_copy(part).wait_recv()
        for upper in range(2):
            for x in range(3):
                columns = slice(384 * x, 384 * x + 384)
                self.pieces[part, upper, x] = (
                    self.ours[part, upper, :, columns]
                    + self.taken[part, upper, :, columns].astype(F32)).astype(BF16)

        @pl.loop(0, 6)
        def _(k):
            mine, copy = self.plane_copy(part, k)
            pl.when(jnp.logical_not(mine))(copy.start)

        @pl.when(self.holds)
        def _():
            self.plane[part, self.me] = self.pieces[part, lax.rem(self.y, 2), self.x]

    def z_copy(self, part, k):
        k = lax.rem(k + self.z, 8)
        block = 4 * part + lax.rem(k, 4)
        to = lax.div(k, 4) * 8 + block
        return to != self.z, pltpu.make_async_remote_copy(
            src_ref=self.z_out.at[block], dst_ref=self.z_in.at[self.z],
            send_sem=self.zs.at[part, k], recv_sem=self.zr.at[self.z],
            device_id=device(self.core, self.x, self.y, to), device_id_type=MESH)

    def z_start(self, part):
        @pl.when(self.holds)
        def _():
            @pl.loop(0, 16)
            def _(k):
                @pl.when(k != self.me)
                def _():
                    block = self.plane.at[part, k]
                    pltpu.make_async_remote_copy(
                        src_ref=block, dst_ref=block, send_sem=self.ps.at[part, 0], recv_sem=self.pr.at[part, k],
                        device_id=device(1 - self.core, self.x, self.y, self.z), device_id_type=MESH).wait_recv()

            for r in range(3):
                rows = slice(24 * r, 24 * r + 24)
                sum_rows = self.plane[part, 0, rows].astype(F32)
                for k in range(1, 16):
                    sum_rows = sum_rows + self.plane[part, k, rows].astype(F32)
                self.total[rows] = sum_rows
            for k in range(4):
                self.z_out[4 * part + k] = self.total[18 * k:18 * k + 18, :].astype(BF16)

            @pl.loop(0, 8)
            def _(k):
                away, copy = self.z_copy(part, k)
                pl.when(away)(copy.start)

            @pl.when(lax.div(lax.rem(self.z, 8), 4) == part)
            def _():
                self.z_in[self.z] = self.z_out[lax.rem(self.z, 8)]

    def x_copy(self, k):
        other = lax.div(k, 4)
        return pltpu.make_async_remote_copy(
            src_ref=self.x_out, dst_ref=self.x_in.at[self.x],
            send_sem=self.xs.at[k], recv_sem=self.xr.at[self.x],
            device_id=device(lax.rem(self.core + other, 2), lax.rem(self.x + k, 4), self.y, self.z),
            device_id_type=MESH)

    def x_start(self):
        @pl.when(self.holds)
        def _():
            @pl.loop(0, 16)
            def _(k):
                @pl.when(k != self.z)
                def _():
                    block = self.z_in.at[k]
                    pltpu.make_async_remote_copy(
                        src_ref=block, dst_ref=block, send_sem=self.zs.at[0, 0], recv_sem=self.zr.at[k],
                        device_id=device(1 - self.core, self.x, self.y, self.z), device_id_type=MESH).wait_recv()

            sum_rows = self.z_in[0].astype(F32)
            for k in range(1, 16):
                sum_rows = sum_rows + self.z_in[k].astype(F32)
            self.x_out[...] = sum_rows.astype(BF16)

            @pl.loop(1, 8)
            def _(k):
                self.x_copy(k).start()

            self.x_in[self.x] = self.x_out[...]

    def finish(self, out):
        for k in range(3):
            @pl.when(jnp.logical_not(jnp.logical_and(self.holds, self.x == k)))
            def _():
                block = self.x_in.at[k]
                pltpu.make_async_remote_copy(
                    src_ref=block, dst_ref=block, send_sem=self.xs.at[0], recv_sem=self.xr.at[k],
                    device_id=device(1 - self.core, self.x, self.y, self.z), device_id_type=MESH).wait_recv()
            out[:, 384 * k:384 * k + 384] = self.x_in[k].astype(F32)

    def drain(self):
        for part in range(2):
            self.core_copy(part).wait_send()

            @pl.loop(0, 6)
            def _(k):
                mine, copy = self.plane_copy(part, k)
                pl.when(jnp.logical_not(mine))(copy.wait_send)

        @pl.when(self.holds)
        def _():
            for part in range(2):
                @pl.loop(0, 8)
                def _(k):
                    away, copy = self.z_copy(part, k)
                    pl.when(away)(copy.wait_send)

            @pl.loop(1, 8)
            def _(k):
                self.x_copy(k).wait_send()


REDUCE_SCRATCH = [
    pltpu.VMEM((2, 2, 72, 1152), BF16),
    pltpu.VMEM((2, 2, 72, 1152), F32),
    pltpu.VMEM((2, 2, 72, 1152), BF16),
    pltpu.VMEM((2, 2, 3, 72, 384), BF16),
    pltpu.VMEM((2, 16, 72, 384), BF16),
    pltpu.VMEM((72, 384), F32),
    pltpu.VMEM((8, 18, 384), BF16),
    pltpu.VMEM((16, 18, 384), BF16),
    pltpu.VMEM((18, 384), BF16),
    pltpu.VMEM((3, 18, 384), BF16),
]
REDUCE_SEMS = [pltpu.SemaphoreType.DMA(n) for n in ((2,), (2,), (2, 6), (2, 16), (2, 8), (16,), (8,), (3,))]


def times(left, right):
    return jnp.dot(left, right, preferred_element_type=F32)


def times_transposed(left, right):
    return lax.dot_general(left, right, (((1,), (1,)), ((), ())), preferred_element_type=F32)


def transposed_times(left, right):
    return lax.dot_general(left, right, (((0,), (0,)), ((), ())), preferred_element_type=F32)


def split_heads(ref, array):
    for h in range(HEADS):
        ref[h] = array[HEAD * h:HEAD * h + HEAD, :]


def attend(head, queries, keys, values, visible, weights, out):
    scores = transposed_times(keys[head], queries[head]) * SCALE
    if visible is not None:
        scores = jnp.where(visible, scores, -1e30)
    powers = jnp.exp(scores - jnp.max(scores, axis=0, keepdims=True))
    share = powers / jnp.sum(powers, axis=0, keepdims=True)
    weights[head] = share
    out[head] = times(values[head], share.astype(BF16)).astype(BF16)


def attend_grad(head, upstream, queries, keys, values, weights, query_grad, key_grad, value_grad):
    upper, share = upstream[head], weights[head]
    share_grad = transposed_times(values[head], upper)
    score_grad = (share * (share_grad - jnp.sum(share_grad * share, axis=0, keepdims=True))).astype(BF16)
    query_grad[head] = (SCALE * times(keys[head], score_grad)).astype(BF16)
    if key_grad is not None:
        value_grad[head] = times_transposed(upper, share.astype(BF16)).astype(BF16)
        key_grad[head] = (SCALE * times_transposed(queries[head], score_grad)).astype(BF16)


def each_head(go):
    for h in range(HEADS):
        go(h)


def block_pair(
    tokens, qkv, text, length, w_os, w_qc, w_oc, w_qkv, cotangent,
    heads_out, tokens_grad, qkv_grad, os_grad, *scratch,
):
    full, landing, sems, scratch = scratch[0:6], scratch[6:12], scratch[12:20], scratch[20:]
    (to_patches, from_frames, to_frames, from_patches, s1_send, s1_recv, s2_send, s2_recv,
     spatial_w, cross_w, temporal_w, mixed_heads, mixed_t, cross_queries, cross_heads, upstream,
     temporal, temporal_up, temporal_heads, temporal_grads, wide_t, half_t, hidden_ref) = scratch[0:23]
    g = Gather((w_os, w_qc, w_oc, w_qkv), landing, full, sems)
    forth = Switch(to_patches, from_frames, s1_send, s1_recv)
    back = Switch(to_frames, from_patches, s2_send, s2_recv)
    r = Reduce(*scratch[23:33], scratch[33:41])

    barrier = pltpu.get_barrier_semaphore()
    greeted = greet(barrier)
    for b in WEIGHTS:
        g.stage(b)
    pl.semaphore_wait(barrier, greeted)

    def whole(w):
        return full[w][...].reshape(-1, COLUMNS[w])

    def join(heads, into=wide_t):
        for h in range(HEADS):
            into[HEAD * h:HEAD * h + HEAD, :] = heads[h]
        return into[...].T

    def in_halves(transposed, array):
        row = lax.broadcasted_iota(jnp.int32, (128, 128), 0)
        token = lax.broadcasted_iota(jnp.int32, (128, 128), 1)
        if transposed:
            row, token = token, row
        from_row = 4 * lax.div(lax.rem(row, 64), 2) + 2 * lax.div(row, 64) + lax.rem(row, 2)
        moves = jnp.where(from_row == token, 1.0, 0.0).astype(BF16)
        return times(moves, array).astype(BF16)

    def spatial_pair(i):
        for h in (2 * i, 2 * i + 1):
            attend(h, qkv.at[0], qkv.at[1], qkv.at[2], None, spatial_w, mixed_heads)

    for w in (OS, QC, OC):
        g.z_start(w)
    for s in range(3):
        spatial_pair(s)
        for w in (OS, QC, OC):
            g.z_step(w, s)
        if s == 1:
            g.z_start(TQ)
    g.z_start(TK)
    g.z_start(TV)
    spatial_pair(3)
    mixed = join(mixed_heads)
    for half in range(2):
        mixed_t[half] = wide_t[288 * half:288 * half + 288, :]
    for w in (OS, QC, OC):
        g.z_step(w, 3)
    g.z_finish(OS)
    g.pack(OS)
    g.z_finish(QC)
    g.pack(QC)
    g.z_finish(OC)
    g.pack(OC)
    for w in (TQ, TK, TV):
        g.z_step(w, 0)
    g.y_step(OS)
    for w in (TQ, TK, TV):
        g.z_step(w, 1)
    g.y_step(QC)
    g.y_last(OS)
    g.y_step(OC)
    g.x_step(OS)
    g.z_step(TQ, 2)
    g.y_last(QC)
    g.z_step(TK, 2)
    g.x_step(QC)
    g.z_step(TV, 2)
    g.x_last(OS)
    g.y_last(OC)
    g.z_step(TQ, 3)
    g.z_finish(TQ)
    g.pack(TQ)
    g.x_step(OC)
    g.x_last(QC)
    g.finish(OS)
    hidden = (tokens[...].astype(F32) + times(mixed, whole(OS))).astype(BF16)
    hidden_ref[...] = hidden
    for w in (TK, TV):
        g.z_step(w, 3)
        g.z_finish(w)
        g.pack(w)
    g.finish(QC)
    g.x_last(OC)
    split_heads(cross_queries, times(hidden, whole(QC)).astype(BF16).T)
    g.y_step(TQ)
    seen = lax.broadcasted_iota(jnp.int32, (128, 128), 0) < length[0]
    each_head(lambda h: attend(h, cross_queries, text.at[0], text.at[1], seen, cross_w, cross_heads))
    g.finish(OC)
    after = (hidden_ref[...].astype(F32) + times(join(cross_heads), whole(OC))).astype(BF16)
    after = in_halves(False, after)
    for half in range(2):
        to_patches[half] = after[64 * half:64 * half + 64, :].reshape(32, 2, 1152)
        forth.start(half)
    g.y_step(TK)
    g.y_last(TQ)
    g.x_step(TQ)
    g.y_step(TV)
    g.y_last(TK)
    g.x_last(TQ)
    g.x_step(TK)
    g.y_last(TV)
    g.x_step(TV)
    g.x_last(TK)
    g.x_last(TV)
    for half in range(2):
        split_heads(temporal_up.at[half], cotangent[:, 2 * half:2 * half + 2, :].reshape(64, 576).T)
    for w in (TQ, TK, TV):
        g.finish(w)

    same = (lax.rem(lax.broadcasted_iota(jnp.int32, (64, 64), 0), 2)
            == lax.rem(lax.broadcasted_iota(jnp.int32, (64, 64), 1), 2))
    for half in range(2):
        forth.wait(half)
        patched = from_frames[half].reshape(64, 1152)
        for i, w in enumerate((TQ, TK, TV)):
            split_heads(temporal.at[i], times(patched, whole(w)).astype(BF16).T)
        for h in range(HEADS):
            attend(h, temporal.at[0], temporal.at[1], temporal.at[2], same, temporal_w, temporal_heads.at[half])
            attend_grad(h, temporal_up.at[half], temporal.at[0], temporal.at[1], temporal.at[2], temporal_w,
                        temporal_grads.at[0], temporal_grads.at[1], temporal_grads.at[2])
        patch_grad = times_transposed(join(temporal_grads.at[0], half_t), whole(TQ))
        for i, w in ((1, TK), (2, TV)):
            patch_grad = patch_grad + times_transposed(join(temporal_grads.at[i], half_t), whole(w))
        to_frames[half] = patch_grad.astype(BF16).reshape(32, 2, 1152)
        back.start(half)
    for half in range(2):
        heads_out[:, 2 * half:2 * half + 2, :] = join(temporal_heads.at[half], half_t).reshape(32, 2, 576)
    g.drain()
    forth.drain()
    back.wait(0)
    back.wait(1)

    after_grad = in_halves(True, from_patches[...].reshape(128, 1152))
    split_heads(upstream, times_transposed(after_grad, whole(OC)).astype(BF16).T)
    each_head(lambda h: attend_grad(
        h, upstream, cross_queries, text.at[0], text.at[1], cross_w, cross_heads, None, None))
    hidden_grad = (after_grad.astype(F32) + times_transposed(join(cross_heads), whole(QC))).astype(BF16)
    tokens_grad[...] = hidden_grad
    r.core_start(mixed_t, hidden_grad)
    split_heads(upstream, times_transposed(hidden_grad, whole(OS)).astype(BF16).T)
    r.plane_start(0)
    r.plane_start(1)
    each_head(lambda h: attend_grad(
        h, upstream, qkv.at[0], qkv.at[1], qkv.at[2], spatial_w, qkv_grad.at[0], qkv_grad.at[1],
        qkv_grad.at[2]))
    r.z_start(0)
    r.z_start(1)
    r.x_start()
    r.finish(os_grad)
    back.drain()
    r.drain()


def hand_on(*refs):
    for k in range(4):
        refs[4 + k][...] = refs[k][...]


def shards(tokens, spatial_qkv, text_kv, text_len, w_os, w_qc, w_oc, w_qkv, cotangent):
    heads = (HEADS, HEAD, 128)
    vmem = pl.BlockSpec(memory_space=pltpu.VMEM)
    dma = pltpu.SemaphoreType.DMA
    results = pl.pallas_call(
        block_pair,
        out_shape=[
            jax.ShapeDtypeStruct((32, 4, 576), BF16),
            jax.ShapeDtypeStruct((128, 1152), BF16),
            jax.ShapeDtypeStruct((3,) + heads, BF16),
            jax.ShapeDtypeStruct((18, 1152), F32),
        ],
        in_specs=[vmem] * 3 + [pl.BlockSpec(memory_space=pltpu.SMEM)] + [vmem] * 5,
        out_specs=[vmem] * 4,
        scratch_shapes=[pltpu.VMEM((4, 8 * rows, columns), BF16) for rows, columns in zip(ROWS, COLUMNS)]
        + [pltpu.VMEM((8, rows, columns), BF16) for rows, columns in zip(ROWS, COLUMNS)]
        + [dma((6, 4))] * 8
        + [pltpu.VMEM((2, 32, 2, 1152), BF16)] * 4 + [dma((2, 32))] * 4
        + [pltpu.VMEM((HEADS, 128, 128), F32)] * 2 + [pltpu.VMEM((HEADS, 64, 64), F32)]
        + [pltpu.VMEM(heads, BF16), pltpu.VMEM((2, 288, 128), BF16)] + [pltpu.VMEM(heads, BF16)] * 3
        + [pltpu.VMEM((k, HEADS, HEAD, 64), BF16) for k in (3, 2, 2, 3)]
        + [pltpu.VMEM((576, 128), BF16), pltpu.VMEM((576, 64), BF16), pltpu.VMEM((128, 1152), BF16)]
        + REDUCE_SCRATCH + REDUCE_SEMS,
        compiler_params=pltpu.CompilerParams(
            collective_id=0, has_side_effects=True, vmem_limit_bytes=56 * 2**20),
        name="block_pair",
    )(
        tokens.reshape(128, 1152),
        jnp.transpose(spatial_qkv[0, 0], (1, 2, 0)).reshape((3,) + heads),
        jnp.transpose(text_kv[0], (1, 2, 0)).reshape((2,) + heads),
        text_len, w_os, w_qc, w_oc, w_qkv,
        cotangent.reshape(32, 4, 576),
    )
    temporal_heads, tokens_grad, qkv_grad, os_grad = pl.pallas_call(
        hand_on,
        out_shape=[jax.ShapeDtypeStruct(r.shape, r.dtype) for r in results],
        in_specs=[vmem] * 4,
        out_specs=[vmem] * 4,
        name="hand_on",
    )(*results)
    return (
        temporal_heads[None],
        tokens_grad[None, None],
        jnp.transpose(qkv_grad.reshape(3, 576, 128), (2, 0, 1))[None, None],
        os_grad,
    )


def solution(mesh):
    placed = (
        P("dp", "seq", None, None),
        P("dp", "seq", None, None, None),
        P("dp", None, None, None),
        P("dp"),
        P("seq", None),
        P("seq", None),
        P("seq", None),
        P("seq", None),
        P("dp", None, "seq", None),
    )
    return jax.shard_map(
        shards,
        mesh=mesh,
        in_specs=placed,
        out_specs=(
            P("dp", None, "seq", None),
            P("dp", "seq", None, None),
            P("dp", "seq", None, None, None),
            P("seq", None),
        ),
        check_vma=False,
    )
```

```python
import math

import jax
import jax.numpy as jnp
from jax import lax
from jax.experimental import pallas as pl
from jax.experimental.pallas import tpu as pltpu
from jax.sharding import PartitionSpec as P

HEADS = 8
HEAD = 72
SCALE = 1.0 / math.sqrt(HEAD)
MESH = pl.DeviceIdType.MESH
BF16 = jnp.bfloat16
F32 = jnp.float32
OS, QC, OC, TQ, TK, TV = WEIGHTS = range(6)
COLUMNS = (1152, 576, 1152, 576, 576, 576)
ROWS = (18, 36, 18, 36, 36, 36)
CUTS = {18: (0, 48, 80, 112, 144), 36: (0, 80, 144, 224, 288)}
FAR_CORE = (1, 1, 1, 0, 0, 0)


def place():
    dp, seq = lax.axis_index("dp"), lax.axis_index("seq")
    return lax.rem(dp, 2), lax.div(dp, 4), lax.div(seq, 8), lax.rem(lax.div(dp, 2), 2) * 8 + lax.rem(seq, 8)


def device(core, x, y, z):
    return ((x * 2 + lax.div(z, 8)) * 2 + core, y * 8 + lax.rem(z, 8))


class Roll:
    def __init__(self, heard):
        self.heard = heard
        core, x, y, z = place()
        along_z = lambda n: device(core, x, y, lax.rem(z + n + 16, 16))
        along_y = lambda n: device(core, x, lax.rem(y + n + 4, 4), z)
        along_x = lambda n: device(core, lax.rem(x + n + 4, 4), y, z)
        other = device(1 - core, x, y, z)
        self.near = (along_z(1), along_z(-1), along_y(1), along_y(-1), along_x(1), along_x(-1), other)
        self.rounds = (
            (along_z(1), along_z(-1)), (along_z(2), along_z(-2)), (along_z(4), along_z(-4)),
            (along_y(1), along_y(-1)), (along_y(2),), (along_x(1), along_x(-1)), (along_x(2),), (other,))

    def greet(self, barrier):
        for d in self.near:
            pl.semaphore_signal(barrier, inc=1, device_id=d, device_id_type=MESH)
        return len(self.near)

    def call(self, k):
        if k:
            pl.semaphore_wait(self.heard.at[k - 1], len(self.rounds[k - 1]))
        if k < len(self.rounds):
            for d in self.rounds[k]:
                pl.semaphore_signal(self.heard.at[k], inc=1, device_id=d, device_id_type=MESH)


class Gather:
    def __init__(self, shards, landing, full, sems):
        self.shards, self.landing, self.full = shards, landing, full
        (self.zs, self.zr, self.ps, self.pr, self.ws, self.wr, self.qs, self.qr) = sems
        core, x, y, z = place()
        self.core, self.x, self.y, self.slot = core, x, y, lax.rem(z, 8)
        self.step = 1 - 2 * core
        self.next_z = device(core, x, y, lax.rem(z + self.step + 16, 16))
        self.next_y = device(core, x, lax.rem(y + self.step + 4, 4), z)
        self.next_x = device(core, lax.rem(x + self.step + 4, 4), y, z)
        self.partner = device(1 - core, x, y, z)
        self.half = lax.rem(x, 2)

    def stage(self, b):
        shard = self.shards[min(b, TQ)]
        first = 576 * max(b - TQ, 0)
        self.landing[b][self.slot] = shard[:, first:first + COLUMNS[b]]

    def block_copy(self, b, s, slot, to, send, recv):
        block = self.landing[b].at[slot]
        return pltpu.make_async_remote_copy(
            src_ref=block, dst_ref=block, send_sem=send.at[b, s], recv_sem=recv.at[b, s],
            device_id=to, device_id_type=MESH)

    def z_copy(self, b, s, slot):
        return self.block_copy(b, s, slot, self.next_z, self.zs, self.zr)

    def pass_copy(self, b, s, slot):
        return self.block_copy(b, s, slot, self.partner, self.ps, self.pr)

    def away(self, steps):
        return lax.rem(self.slot - steps * self.step + 8, 8)

    def z_start(self, b):
        self.z_copy(b, 0, self.slot).start()

    def z_step(self, b, s):
        def go():
            slot = self.away(s + 1)
            self.z_copy(b, s, slot).wait_recv()
            if s < 2:
                self.z_copy(b, s + 1, slot).start()
            if s == 2:
                pl.when(self.core == FAR_CORE[b])(lambda: self.z_copy(b, 3, slot).start())
            self.pass_copy(b, s, slot).start()

        if s < 3:
            go()
        else:
            pl.when(self.core == FAR_CORE[b])(go)

    def z_finish(self, b):
        for s in range(3):
            self.pass_copy(b, s, lax.rem(self.slot + (s + 1) * self.step + 8, 8)).wait_recv()
        pl.when(self.core != FAR_CORE[b])(
            lambda: self.pass_copy(b, 3, lax.rem(self.slot + 4, 8)).wait_recv())

    def pack(self, w):
        rows = ROWS[w]
        for k in range(8):
            self.full[w][self.y, k * rows:(k + 1) * rows, :] = self.landing[w][k]
        self.by_half(w, self.half, lambda c: c(self.y, None, self.next_y, 0, self.ws, self.wr).start())

    def part_copy(self, w, half, share, quarter, to, s, send, recv):
        cuts = CUTS[ROWS[w]]
        first, last = (cuts[2 * half], cuts[2 * half + 2]) if share is None else (
            cuts[2 * half + share], cuts[2 * half + share + 1])
        block = self.full[w].at[quarter, pl.ds(first, last - first)]
        return pltpu.make_async_remote_copy(
            src_ref=block, dst_ref=block, send_sem=send.at[w, s], recv_sem=recv.at[w, s],
            device_id=to, device_id_type=MESH)

    def by_half(self, w, half, go):
        for h in range(2):
            @pl.when(half == h)
            def _():
                go(lambda quarter, share, to, s, send, recv: self.part_copy(
                    w, h, share, quarter, to, s, send, recv))

    def by_share(self, w, half, share, go):
        for c in range(2):
            @pl.when(share == c)
            def _():
                self.by_half(w, half, lambda copy: go(lambda quarter, to, s, send, recv: copy(
                    quarter, c, to, s, send, recv)))

    def near(self):
        return lax.rem(self.y - self.step + 4, 4)

    def far(self):
        return lax.rem(self.y + 2, 4)

    def y_step(self, w):
        def near(copy):
            copy(self.near(), None, self.next_y, 0, self.ws, self.wr).wait_recv()
            copy(self.near(), None, self.next_x, 2, self.ws, self.wr).start()
            copy(self.near(), None, self.partner, 0, self.qs, self.qr).start()

        self.by_half(w, self.half, near)
        self.by_share(w, self.half, self.core, lambda copy: copy(
            self.near(), self.next_y, 1, self.ws, self.wr).start())

    def y_last(self, w):
        def far(copy):
            copy(self.far(), self.next_y, 1, self.ws, self.wr).wait_recv()
            copy(self.far(), self.next_x, 3, self.ws, self.wr).start()
            copy(self.far(), self.partner, 1, self.qs, self.qr).start()

        self.by_share(w, self.half, self.core, far)

    def x_step(self, w):
        def near(copy):
            copy(self.near(), None, self.next_x, 2, self.ws, self.wr).wait_recv()
            copy(self.near(), None, self.partner, 2, self.qs, self.qr).start()

        self.by_half(w, 1 - self.half, near)

    def x_last(self, w):
        def far(copy):
            copy(self.far(), self.next_x, 3, self.ws, self.wr).wait_recv()
            copy(self.far(), self.partner, 3, self.qs, self.qr).start()

        self.by_share(w, 1 - self.half, self.core, far)

    def finish(self, w):
        other = lax.rem(self.y + self.step + 4, 4)
        self.by_half(w, self.half, lambda copy: copy(
            other, None, self.partner, 0, self.qs, self.qr).wait_recv())
        self.by_half(w, 1 - self.half, lambda copy: copy(
            other, None, self.partner, 2, self.qs, self.qr).wait_recv())
        self.by_share(w, self.half, 1 - self.core, lambda copy: copy(
            self.far(), self.partner, 1, self.qs, self.qr).wait_recv())
        self.by_share(w, 1 - self.half, 1 - self.core, lambda copy: copy(
            self.far(), self.partner, 3, self.qs, self.qr).wait_recv())

    def drain(self):
        for b in WEIGHTS:
            for s in range(3):
                self.z_copy(b, s, self.away(s)).wait_send()
                self.pass_copy(b, s, self.away(s + 1)).wait_send()

            @pl.when(self.core == FAR_CORE[b])
            def _():
                self.z_copy(b, 3, self.away(3)).wait_send()
                self.pass_copy(b, 3, self.away(4)).wait_send()

        for w in WEIGHTS:
            def mine(copy):
                copy(self.y, None, self.next_y, 0, self.ws, self.wr).wait_send()
                copy(self.near(), None, self.next_x, 2, self.ws, self.wr).wait_send()
                copy(self.near(), None, self.partner, 0, self.qs, self.qr).wait_send()

            def mine_far(copy):
                copy(self.near(), self.next_y, 1, self.ws, self.wr).wait_send()
                copy(self.far(), self.next_x, 3, self.ws, self.wr).wait_send()
                copy(self.far(), self.partner, 1, self.qs, self.qr).wait_send()

            self.by_half(w, self.half, mine)
            self.by_half(w, 1 - self.half, lambda copy: copy(
                self.near(), None, self.partner, 2, self.qs, self.qr).wait_send())
            self.by_share(w, self.half, self.core, mine_far)
            self.by_share(w, 1 - self.half, self.core, lambda copy: copy(
                self.far(), self.partner, 3, self.qs, self.qr).wait_send())


class Switch:
    def __init__(self, out, taken, send, recv):
        self.out, self.taken, self.send, self.recv = out, taken, send, recv
        self.dp, self.seq = lax.axis_index("dp"), lax.axis_index("seq")

    def copy(self, half, k):
        to = lax.rem(self.seq + k, 32)
        return pltpu.make_async_remote_copy(
            src_ref=self.out.at[half, to], dst_ref=self.taken.at[half, self.seq],
            send_sem=self.send.at[half, k], recv_sem=self.recv.at[half, k],
            device_id=(self.dp, to), device_id_type=MESH)

    def start(self, half):
        @pl.loop(1, 32)
        def _(k):
            self.copy(half, k).start()

        self.taken[half, self.seq] = self.out[half, self.seq]

    def wait(self, half):
        @pl.loop(1, 32)
        def _(k):
            block = self.taken.at[half, lax.rem(self.seq - k + 32, 32)]
            pltpu.make_async_remote_copy(
                src_ref=block, dst_ref=block, send_sem=self.send.at[half, k], recv_sem=self.recv.at[half, k],
                device_id=(self.dp, lax.rem(self.seq + k, 32)), device_id_type=MESH).wait_recv()

    def drain(self):
        for half in range(2):
            @pl.loop(1, 32)
            def _(k):
                self.copy(half, k).wait_send()


class Reduce:
    def __init__(self, theirs, ours, taken, pieces, plane, total, z_out, z_in, x_out, x_in, sems):
        self.theirs, self.ours, self.taken, self.pieces, self.plane = theirs, ours, taken, pieces, plane
        self.total, self.z_out, self.z_in, self.x_out, self.x_in = total, z_out, z_in, x_out, x_in
        (self.cs, self.cr, self.ps, self.pr, self.zs, self.zr, self.xs, self.xr) = sems
        self.core, self.x, self.y, self.z = place()
        self.holds = jnp.logical_and(self.x < 3, lax.div(self.y, 2) == self.core)
        self.me = self.x * 4 + self.y

    def core_copy(self, part):
        return pltpu.make_async_remote_copy(
            src_ref=self.theirs.at[part], dst_ref=self.taken.at[part],
            send_sem=self.cs.at[part], recv_sem=self.cr.at[part],
            device_id=device(1 - self.core, self.x, self.y, self.z), device_id_type=MESH)

    def core_start(self, mixed_t, grad):
        half = times(mixed_t[1 - self.core], grad)
        for part in range(2):
            for upper in range(2):
                at = 144 * upper + 72 * part
                self.theirs[part, upper] = half[at:at + 72].astype(BF16)
            self.core_copy(part).start()
        half = times(mixed_t[self.core], grad)
        for part in range(2):
            for upper in range(2):
                at = 144 * upper + 72 * part
                self.ours[part, upper] = half[at:at + 72]

    def plane_copy(self, part, k):
        piece = lax.rem(k + self.x + 2 * self.y, 6)
        upper, x = lax.div(piece, 3), lax.rem(piece, 3)
        mine = jnp.logical_and(self.x == x, self.y == self.core * 2 + upper)
        copy = pltpu.make_async_remote_copy(
            src_ref=self.pieces.at[part, upper, x], dst_ref=self.plane.at[part, self.me],
            send_sem=self.ps.at[part, k], recv_sem=self.pr.at[part, self.me],
            device_id=device(self.core, x, self.core * 2 + upper, self.z), device_id_type=MESH)
        return mine, copy

    def plane_start(self, part):
        self.core_copy(part).wait_recv()
        for upper in range(2):
            for x in range(3):
                columns = slice(384 * x, 384 * x + 384)
                self.pieces[part, upper, x] = (
                    self.ours[part, upper, :, columns]
                    + self.taken[part, upper, :, columns].astype(F32)).astype(BF16)

        @pl.loop(0, 6)
        def _(k):
            mine, copy = self.plane_copy(part, k)
            pl.when(jnp.logical_not(mine))(copy.start)

        @pl.when(self.holds)
        def _():
            self.plane[part, self.me] = self.pieces[part, lax.rem(self.y, 2), self.x]

    def z_copy(self, part, k):
        k = lax.rem(k + self.z, 8)
        block = 4 * part + lax.rem(k, 4)
        to = lax.div(k, 4) * 8 + block
        return to != self.z, pltpu.make_async_remote_copy(
            src_ref=self.z_out.at[block], dst_ref=self.z_in.at[self.z],
            send_sem=self.zs.at[part, k], recv_sem=self.zr.at[self.z],
            device_id=device(self.core, self.x, self.y, to), device_id_type=MESH)

    def z_start(self, part):
        @pl.when(self.holds)
        def _():
            @pl.loop(0, 16)
            def _(k):
                @pl.when(k != self.me)
                def _():
                    block = self.plane.at[part, k]
                    pltpu.make_async_remote_copy(
                        src_ref=block, dst_ref=block, send_sem=self.ps.at[part, 0], recv_sem=self.pr.at[part, k],
                        device_id=device(1 - self.core, self.x, self.y, self.z), device_id_type=MESH).wait_recv()

            for r in range(3):
                rows = slice(24 * r, 24 * r + 24)
                sum_rows = self.plane[part, 0, rows].astype(F32)
                for k in range(1, 16):
                    sum_rows = sum_rows + self.plane[part, k, rows].astype(F32)
                self.total[rows] = sum_rows
            for k in range(4):
                self.z_out[4 * part + k] = self.total[18 * k:18 * k + 18, :].astype(BF16)

            @pl.loop(0, 8)
            def _(k):
                away, copy = self.z_copy(part, k)
                pl.when(away)(copy.start)

            @pl.when(lax.div(lax.rem(self.z, 8), 4) == part)
            def _():
                self.z_in[self.z] = self.z_out[lax.rem(self.z, 8)]

    def x_copy(self, k):
        other = lax.div(k, 4)
        return pltpu.make_async_remote_copy(
            src_ref=self.x_out, dst_ref=self.x_in.at[self.x],
            send_sem=self.xs.at[k], recv_sem=self.xr.at[self.x],
            device_id=device(lax.rem(self.core + other, 2), lax.rem(self.x + k, 4), self.y, self.z),
            device_id_type=MESH)

    def x_start(self):
        @pl.when(self.holds)
        def _():
            @pl.loop(0, 16)
            def _(k):
                @pl.when(k != self.z)
                def _():
                    block = self.z_in.at[k]
                    pltpu.make_async_remote_copy(
                        src_ref=block, dst_ref=block, send_sem=self.zs.at[0, 0], recv_sem=self.zr.at[k],
                        device_id=device(1 - self.core, self.x, self.y, self.z), device_id_type=MESH).wait_recv()

            sum_rows = self.z_in[0].astype(F32)
            for k in range(1, 16):
                sum_rows = sum_rows + self.z_in[k].astype(F32)
            self.x_out[...] = sum_rows.astype(BF16)

            @pl.loop(1, 8)
            def _(k):
                self.x_copy(k).start()

            self.x_in[self.x] = self.x_out[...]

    def finish(self, out):
        for k in range(3):
            @pl.when(jnp.logical_not(jnp.logical_and(self.holds, self.x == k)))
            def _():
                block = self.x_in.at[k]
                pltpu.make_async_remote_copy(
                    src_ref=block, dst_ref=block, send_sem=self.xs.at[0], recv_sem=self.xr.at[k],
                    device_id=device(1 - self.core, self.x, self.y, self.z), device_id_type=MESH).wait_recv()
            out[:, 384 * k:384 * k + 384] = self.x_in[k].astype(F32)

    def drain(self):
        for part in range(2):
            self.core_copy(part).wait_send()

            @pl.loop(0, 6)
            def _(k):
                mine, copy = self.plane_copy(part, k)
                pl.when(jnp.logical_not(mine))(copy.wait_send)

        @pl.when(self.holds)
        def _():
            for part in range(2):
                @pl.loop(0, 8)
                def _(k):
                    away, copy = self.z_copy(part, k)
                    pl.when(away)(copy.wait_send)

            @pl.loop(1, 8)
            def _(k):
                self.x_copy(k).wait_send()


REDUCE_SCRATCH = [
    pltpu.VMEM((2, 2, 72, 1152), BF16),
    pltpu.VMEM((2, 2, 72, 1152), F32),
    pltpu.VMEM((2, 2, 72, 1152), BF16),
    pltpu.VMEM((2, 2, 3, 72, 384), BF16),
    pltpu.VMEM((2, 16, 72, 384), BF16),
    pltpu.VMEM((72, 384), F32),
    pltpu.VMEM((8, 18, 384), BF16),
    pltpu.VMEM((16, 18, 384), BF16),
    pltpu.VMEM((18, 384), BF16),
    pltpu.VMEM((3, 18, 384), BF16),
]
REDUCE_SEMS = [pltpu.SemaphoreType.DMA(n) for n in ((2,), (2,), (2, 6), (2, 16), (2, 8), (16,), (8,), (3,))]


def times(left, right):
    return jnp.dot(left, right, preferred_element_type=F32)


def times_transposed(left, right):
    return lax.dot_general(left, right, (((1,), (1,)), ((), ())), preferred_element_type=F32)


def transposed_times(left, right):
    return lax.dot_general(left, right, (((0,), (0,)), ((), ())), preferred_element_type=F32)


def split_heads(ref, array):
    for h in range(HEADS):
        ref[h] = array[HEAD * h:HEAD * h + HEAD, :]


def attend(head, queries, keys, values, visible, weights, out):
    scores = transposed_times(keys[head], queries[head]) * SCALE
    if visible is not None:
        scores = jnp.where(visible, scores, -1e30)
    powers = jnp.exp(scores - jnp.max(scores, axis=0, keepdims=True))
    share = powers / jnp.sum(powers, axis=0, keepdims=True)
    weights[head] = share
    out[head] = times(values[head], share.astype(BF16)).astype(BF16)


def attend_grad(head, upstream, queries, keys, values, weights, query_grad, key_grad, value_grad):
    upper, share = upstream[head], weights[head]
    share_grad = transposed_times(values[head], upper)
    score_grad = (share * (share_grad - jnp.sum(share_grad * share, axis=0, keepdims=True))).astype(BF16)
    query_grad[head] = (SCALE * times(keys[head], score_grad)).astype(BF16)
    if key_grad is not None:
        value_grad[head] = times_transposed(upper, share.astype(BF16)).astype(BF16)
        key_grad[head] = (SCALE * times_transposed(queries[head], score_grad)).astype(BF16)


def each_head(go):
    for h in range(HEADS):
        go(h)


def block_pair(
    tokens, qkv, text, length, w_os, w_qc, w_oc, w_qkv, cotangent,
    heads_out, tokens_grad, qkv_grad, os_grad, *scratch,
):
    full, landing, sems, scratch = scratch[0:6], scratch[6:12], scratch[12:20], scratch[20:]
    (to_patches, from_frames, to_frames, from_patches, s1_send, s1_recv, s2_send, s2_recv,
     spatial_w, cross_w, temporal_w, mixed_heads, mixed_t, cross_queries, cross_heads, upstream,
     temporal, temporal_up, temporal_heads, temporal_grads, wide_t, half_t, hidden_ref) = scratch[0:23]
    g = Gather((w_os, w_qc, w_oc, w_qkv), landing, full, sems)
    forth = Switch(to_patches, from_frames, s1_send, s1_recv)
    back = Switch(to_frames, from_patches, s2_send, s2_recv)
    r = Reduce(*scratch[23:33], scratch[33:41])

    barrier = pltpu.get_barrier_semaphore()
    roll = Roll(scratch[41])
    greeted = roll.greet(barrier)
    for b in WEIGHTS:
        g.stage(b)
    pl.semaphore_wait(barrier, greeted)

    def whole(w):
        return full[w][...].reshape(-1, COLUMNS[w])

    def join(heads, into=wide_t):
        for h in range(HEADS):
            into[HEAD * h:HEAD * h + HEAD, :] = heads[h]
        return into[...].T

    def in_halves(transposed, array):
        row = lax.broadcasted_iota(jnp.int32, (128, 128), 0)
        token = lax.broadcasted_iota(jnp.int32, (128, 128), 1)
        if transposed:
            row, token = token, row
        from_row = 4 * lax.div(lax.rem(row, 64), 2) + 2 * lax.div(row, 64) + lax.rem(row, 2)
        moves = jnp.where(from_row == token, 1.0, 0.0).astype(BF16)
        return times(moves, array).astype(BF16)

    def spatial_pair(i):
        for h in (2 * i, 2 * i + 1):
            attend(h, qkv.at[0], qkv.at[1], qkv.at[2], None, spatial_w, mixed_heads)

    for w in (OS, QC, OC):
        g.z_start(w)
    roll.call(0)
    for s in range(3):
        spatial_pair(s)
        for w in (OS, QC, OC):
            g.z_step(w, s)
        roll.call(s + 1)
        if s == 1:
            g.z_start(TQ)
    g.z_start(TK)
    g.z_start(TV)
    spatial_pair(3)
    mixed = join(mixed_heads)
    for half in range(2):
        mixed_t[half] = wide_t[288 * half:288 * half + 288, :]
    for w in (OS, QC, OC):
        g.z_step(w, 3)
    g.z_finish(OS)
    g.pack(OS)
    g.z_finish(QC)
    g.pack(QC)
    g.z_finish(OC)
    g.pack(OC)
    roll.call(4)
    for w in (TQ, TK, TV):
        g.z_step(w, 0)
    g.y_step(OS)
    for w in (TQ, TK, TV):
        g.z_step(w, 1)
    g.y_step(QC)
    roll.call(5)
    g.y_last(OS)
    g.y_step(OC)
    g.x_step(OS)
    roll.call(6)
    g.z_step(TQ, 2)
    g.y_last(QC)
    g.z_step(TK, 2)
    g.x_step(QC)
    roll.call(7)
    g.z_step(TV, 2)
    g.x_last(OS)
    g.y_last(OC)
    g.z_step(TQ, 3)
    g.z_finish(TQ)
    g.pack(TQ)
    g.x_step(OC)
    g.x_last(QC)
    g.finish(OS)
    hidden = (tokens[...].astype(F32) + times(mixed, whole(OS))).astype(BF16)
    hidden_ref[...] = hidden
    for w in (TK, TV):
        g.z_step(w, 3)
        g.z_finish(w)
        g.pack(w)
    g.finish(QC)
    roll.call(8)
    g.x_last(OC)
    split_heads(cross_queries, times(hidden, whole(QC)).astype(BF16).T)
    g.y_step(TQ)
    seen = lax.broadcasted_iota(jnp.int32, (128, 128), 0) < length[0]
    each_head(lambda h: attend(h, cross_queries, text.at[0], text.at[1], seen, cross_w, cross_heads))
    g.finish(OC)
    after = (hidden_ref[...].astype(F32) + times(join(cross_heads), whole(OC))).astype(BF16)
    after = in_halves(False, after)
    for half in range(2):
        to_patches[half] = after[64 * half:64 * half + 64, :].reshape(32, 2, 1152)
        forth.start(half)
    g.y_step(TK)
    g.y_last(TQ)
    g.x_step(TQ)
    g.y_step(TV)
    g.y_last(TK)
    g.x_last(TQ)
    g.x_step(TK)
    g.y_last(TV)
    g.x_step(TV)
    g.x_last(TK)
    g.x_last(TV)
    for half in range(2):
        split_heads(temporal_up.at[half], cotangent[:, 2 * half:2 * half + 2, :].reshape(64, 576).T)
    for w in (TQ, TK, TV):
        g.finish(w)

    same = (lax.rem(lax.broadcasted_iota(jnp.int32, (64, 64), 0), 2)
            == lax.rem(lax.broadcasted_iota(jnp.int32, (64, 64), 1), 2))
    for half in range(2):
        forth.wait(half)
        patched = from_frames[half].reshape(64, 1152)
        for i, w in enumerate((TQ, TK, TV)):
            split_heads(temporal.at[i], times(patched, whole(w)).astype(BF16).T)
        for h in range(HEADS):
            attend(h, temporal.at[0], temporal.at[1], temporal.at[2], same, temporal_w, temporal_heads.at[half])
            attend_grad(h, temporal_up.at[half], temporal.at[0], temporal.at[1], temporal.at[2], temporal_w,
                        temporal_grads.at[0], temporal_grads.at[1], temporal_grads.at[2])
        patch_grad = times_transposed(join(temporal_grads.at[0], half_t), whole(TQ))
        for i, w in ((1, TK), (2, TV)):
            patch_grad = patch_grad + times_transposed(join(temporal_grads.at[i], half_t), whole(w))
        to_frames[half] = patch_grad.astype(BF16).reshape(32, 2, 1152)
        back.start(half)
    for half in range(2):
        heads_out[:, 2 * half:2 * half + 2, :] = join(temporal_heads.at[half], half_t).reshape(32, 2, 576)
    g.drain()
    forth.drain()
    back.wait(0)
    back.wait(1)

    after_grad = in_halves(True, from_patches[...].reshape(128, 1152))
    split_heads(upstream, times_transposed(after_grad, whole(OC)).astype(BF16).T)
    each_head(lambda h: attend_grad(
        h, upstream, cross_queries, text.at[0], text.at[1], cross_w, cross_heads, None, None))
    hidden_grad = (after_grad.astype(F32) + times_transposed(join(cross_heads), whole(QC))).astype(BF16)
    tokens_grad[...] = hidden_grad
    r.core_start(mixed_t, hidden_grad)
    split_heads(upstream, times_transposed(hidden_grad, whole(OS)).astype(BF16).T)
    r.plane_start(0)
    r.plane_start(1)
    each_head(lambda h: attend_grad(
        h, upstream, qkv.at[0], qkv.at[1], qkv.at[2], spatial_w, qkv_grad.at[0], qkv_grad.at[1],
        qkv_grad.at[2]))
    r.z_start(0)
    r.z_start(1)
    r.x_start()
    r.finish(os_grad)
    back.drain()
    r.drain()


def hand_on(*refs):
    for k in range(4):
        refs[4 + k][...] = refs[k][...]


def shards(tokens, spatial_qkv, text_kv, text_len, w_os, w_qc, w_oc, w_qkv, cotangent):
    heads = (HEADS, HEAD, 128)
    vmem = pl.BlockSpec(memory_space=pltpu.VMEM)
    dma = pltpu.SemaphoreType.DMA
    results = pl.pallas_call(
        block_pair,
        out_shape=[
            jax.ShapeDtypeStruct((32, 4, 576), BF16),
            jax.ShapeDtypeStruct((128, 1152), BF16),
            jax.ShapeDtypeStruct((3,) + heads, BF16),
            jax.ShapeDtypeStruct((18, 1152), F32),
        ],
        in_specs=[vmem] * 3 + [pl.BlockSpec(memory_space=pltpu.SMEM)] + [vmem] * 5,
        out_specs=[vmem] * 4,
        scratch_shapes=[pltpu.VMEM((4, 8 * rows, columns), BF16) for rows, columns in zip(ROWS, COLUMNS)]
        + [pltpu.VMEM((8, rows, columns), BF16) for rows, columns in zip(ROWS, COLUMNS)]
        + [dma((6, 4))] * 8
        + [pltpu.VMEM((2, 32, 2, 1152), BF16)] * 4 + [dma((2, 32))] * 4
        + [pltpu.VMEM((HEADS, 128, 128), F32)] * 2 + [pltpu.VMEM((HEADS, 64, 64), F32)]
        + [pltpu.VMEM(heads, BF16), pltpu.VMEM((2, 288, 128), BF16)] + [pltpu.VMEM(heads, BF16)] * 3
        + [pltpu.VMEM((k, HEADS, HEAD, 64), BF16) for k in (3, 2, 2, 3)]
        + [pltpu.VMEM((576, 128), BF16), pltpu.VMEM((576, 64), BF16), pltpu.VMEM((128, 1152), BF16)]
        + REDUCE_SCRATCH + REDUCE_SEMS + [pltpu.SemaphoreType.REGULAR((8,))],
        compiler_params=pltpu.CompilerParams(
            collective_id=0, has_side_effects=True, vmem_limit_bytes=56 * 2**20),
        name="block_pair",
    )(
        tokens.reshape(128, 1152),
        jnp.transpose(spatial_qkv[0, 0], (1, 2, 0)).reshape((3,) + heads),
        jnp.transpose(text_kv[0], (1, 2, 0)).reshape((2,) + heads),
        text_len, w_os, w_qc, w_oc, w_qkv,
        cotangent.reshape(32, 4, 576),
    )
    temporal_heads, tokens_grad, qkv_grad, os_grad = pl.pallas_call(
        hand_on,
        out_shape=[jax.ShapeDtypeStruct(r.shape, r.dtype) for r in results],
        in_specs=[vmem] * 4,
        out_specs=[vmem] * 4,
        name="hand_on",
    )(*results)
    return (
        temporal_heads[None],
        tokens_grad[None, None],
        jnp.transpose(qkv_grad.reshape(3, 576, 128), (2, 0, 1))[None, None],
        os_grad,
    )


def solution(mesh):
    placed = (
        P("dp", "seq", None, None),
        P("dp", "seq", None, None, None),
        P("dp", None, None, None),
        P("dp"),
        P("seq", None),
        P("seq", None),
        P("seq", None),
        P("seq", None),
        P("dp", None, "seq", None),
    )
    return jax.shard_map(
        shards,
        mesh=mesh,
        in_specs=placed,
        out_specs=(
            P("dp", None, "seq", None),
            P("dp", "seq", None, None),
            P("dp", "seq", None, None, None),
            P("seq", None),
        ),
        check_vma=False,
    )
```

```python
import math

import jax
import jax.numpy as jnp
from jax import lax
from jax.experimental import pallas as pl
from jax.experimental.pallas import tpu as pltpu
from jax.sharding import PartitionSpec as P

HEADS = 8
HEAD = 72
SCALE = 1.0 / math.sqrt(HEAD)
MESH = pl.DeviceIdType.MESH
BF16 = jnp.bfloat16
F32 = jnp.float32
OS, QC, OC, TQ, TK, TV = WEIGHTS = range(6)
COLUMNS = (1152, 576, 1152, 576, 576, 576)
ROWS = (18, 36, 18, 36, 36, 36)
CUTS = {18: (0, 48, 80, 112, 144), 36: (0, 80, 144, 224, 288)}
FAR_CORE = (1, 1, 1, 0, 0, 0)


def place():
    dp, seq = lax.axis_index("dp"), lax.axis_index("seq")
    return lax.rem(dp, 2), lax.div(dp, 4), lax.div(seq, 8), lax.rem(lax.div(dp, 2), 2) * 8 + lax.rem(seq, 8)


def device(core, x, y, z):
    return ((x * 2 + lax.div(z, 8)) * 2 + core, y * 8 + lax.rem(z, 8))


class Roll:
    def __init__(self, heard):
        self.heard = heard
        core, x, y, z = place()
        along_z = lambda n: device(core, x, y, lax.rem(z + n + 16, 16))
        along_y = lambda n: device(core, x, lax.rem(y + n + 4, 4), z)
        along_x = lambda n: device(core, lax.rem(x + n + 4, 4), y, z)
        other = device(1 - core, x, y, z)
        self.near = (along_z(1), along_z(-1), along_y(1), along_y(-1), along_x(1), along_x(-1), other)
        self.rounds = (
            (along_z(1), along_z(-1)), (along_z(2), along_z(-2)), (along_z(4), along_z(-4)),
            (along_y(1), along_y(-1)), (along_y(2),), (along_x(1), along_x(-1)), (along_x(2),), (other,))

    def greet(self, barrier):
        for d in self.near:
            pl.semaphore_signal(barrier, inc=1, device_id=d, device_id_type=MESH)
        return len(self.near)

    def call(self, k):
        if k:
            pl.semaphore_wait(self.heard.at[k - 1], len(self.rounds[k - 1]))
        if k < len(self.rounds):
            for d in self.rounds[k]:
                pl.semaphore_signal(self.heard.at[k], inc=1, device_id=d, device_id_type=MESH)


class Gather:
    def __init__(self, shards, landing, full, sems):
        self.shards, self.landing, self.full = shards, landing, full
        (self.zs, self.zr, self.ps, self.pr, self.ws, self.wr, self.qs, self.qr) = sems
        core, x, y, z = place()
        self.core, self.x, self.y, self.slot = core, x, y, lax.rem(z, 8)
        self.step = 1 - 2 * core
        self.next_z = device(core, x, y, lax.rem(z + self.step + 16, 16))
        self.next_y = device(core, x, lax.rem(y + self.step + 4, 4), z)
        self.next_x = device(core, lax.rem(x + self.step + 4, 4), y, z)
        self.partner = device(1 - core, x, y, z)
        self.half = lax.rem(x, 2)

    def stage(self, b):
        shard = self.shards[min(b, TQ)]
        first = 576 * max(b - TQ, 0)
        self.landing[b][self.slot] = shard[:, first:first + COLUMNS[b]]

    def block_copy(self, b, s, slot, to, send, recv):
        block = self.landing[b].at[slot]
        return pltpu.make_async_remote_copy(
            src_ref=block, dst_ref=block, send_sem=send.at[b, s], recv_sem=recv.at[b, s],
            device_id=to, device_id_type=MESH)

    def z_copy(self, b, s, slot):
        return self.block_copy(b, s, slot, self.next_z, self.zs, self.zr)

    def pass_copy(self, b, s, slot):
        return self.block_copy(b, s, slot, self.partner, self.ps, self.pr)

    def away(self, steps):
        return lax.rem(self.slot - steps * self.step + 8, 8)

    def z_start(self, b):
        self.z_copy(b, 0, self.slot).start()

    def z_step(self, b, s):
        def go():
            slot = self.away(s + 1)
            self.z_copy(b, s, slot).wait_recv()
            if s < 2:
                self.z_copy(b, s + 1, slot).start()
            if s == 2:
                pl.when(self.core == FAR_CORE[b])(lambda: self.z_copy(b, 3, slot).start())
            self.pass_copy(b, s, slot).start()

        if s < 3:
            go()
        else:
            pl.when(self.core == FAR_CORE[b])(go)

    def z_finish(self, b):
        for s in range(3):
            self.pass_copy(b, s, lax.rem(self.slot + (s + 1) * self.step + 8, 8)).wait_recv()
        pl.when(self.core != FAR_CORE[b])(
            lambda: self.pass_copy(b, 3, lax.rem(self.slot + 4, 8)).wait_recv())

    def pack(self, w):
        rows = ROWS[w]
        for k in range(8):
            self.full[w][self.y, k * rows:(k + 1) * rows, :] = self.landing[w][k]
        self.by_half(w, self.half, lambda c: c(self.y, None, self.next_y, 0, self.ws, self.wr).start())

    def part_copy(self, w, half, share, quarter, to, s, send, recv):
        cuts = CUTS[ROWS[w]]
        first, last = (cuts[2 * half], cuts[2 * half + 2]) if share is None else (
            cuts[2 * half + share], cuts[2 * half + share + 1])
        block = self.full[w].at[quarter, pl.ds(first, last - first)]
        return pltpu.make_async_remote_copy(
            src_ref=block, dst_ref=block, send_sem=send.at[w, s], recv_sem=recv.at[w, s],
            device_id=to, device_id_type=MESH)

    def by_half(self, w, half, go):
        for h in range(2):
            @pl.when(half == h)
            def _():
                go(lambda quarter, share, to, s, send, recv: self.part_copy(
                    w, h, share, quarter, to, s, send, recv))

    def by_share(self, w, half, share, go):
        for c in range(2):
            @pl.when(share == c)
            def _():
                self.by_half(w, half, lambda copy: go(lambda quarter, to, s, send, recv: copy(
                    quarter, c, to, s, send, recv)))

    def near(self):
        return lax.rem(self.y - self.step + 4, 4)

    def far(self):
        return lax.rem(self.y + 2, 4)

    def y_step(self, w):
        def near(copy):
            copy(self.near(), None, self.next_y, 0, self.ws, self.wr).wait_recv()
            copy(self.near(), None, self.next_x, 2, self.ws, self.wr).start()
            copy(self.near(), None, self.partner, 0, self.qs, self.qr).start()

        self.by_half(w, self.half, near)
        self.by_share(w, self.half, self.core, lambda copy: copy(
            self.near(), self.next_y, 1, self.ws, self.wr).start())

    def y_last(self, w):
        def far(copy):
            copy(self.far(), self.next_y, 1, self.ws, self.wr).wait_recv()
            copy(self.far(), self.next_x, 3, self.ws, self.wr).start()
            copy(self.far(), self.partner, 1, self.qs, self.qr).start()

        self.by_share(w, self.half, self.core, far)

    def x_step(self, w):
        def near(copy):
            copy(self.near(), None, self.next_x, 2, self.ws, self.wr).wait_recv()
            copy(self.near(), None, self.partner, 2, self.qs, self.qr).start()

        self.by_half(w, 1 - self.half, near)

    def x_last(self, w):
        def far(copy):
            copy(self.far(), self.next_x, 3, self.ws, self.wr).wait_recv()
            copy(self.far(), self.partner, 3, self.qs, self.qr).start()

        self.by_share(w, 1 - self.half, self.core, far)

    def finish(self, w):
        other = lax.rem(self.y + self.step + 4, 4)
        self.by_half(w, self.half, lambda copy: copy(
            other, None, self.partner, 0, self.qs, self.qr).wait_recv())
        self.by_half(w, 1 - self.half, lambda copy: copy(
            other, None, self.partner, 2, self.qs, self.qr).wait_recv())
        self.by_share(w, self.half, 1 - self.core, lambda copy: copy(
            self.far(), self.partner, 1, self.qs, self.qr).wait_recv())
        self.by_share(w, 1 - self.half, 1 - self.core, lambda copy: copy(
            self.far(), self.partner, 3, self.qs, self.qr).wait_recv())

    def drain(self):
        for b in WEIGHTS:
            for s in range(3):
                self.z_copy(b, s, self.away(s)).wait_send()
                self.pass_copy(b, s, self.away(s + 1)).wait_send()

            @pl.when(self.core == FAR_CORE[b])
            def _():
                self.z_copy(b, 3, self.away(3)).wait_send()
                self.pass_copy(b, 3, self.away(4)).wait_send()

        for w in WEIGHTS:
            def mine(copy):
                copy(self.y, None, self.next_y, 0, self.ws, self.wr).wait_send()
                copy(self.near(), None, self.next_x, 2, self.ws, self.wr).wait_send()
                copy(self.near(), None, self.partner, 0, self.qs, self.qr).wait_send()

            def mine_far(copy):
                copy(self.near(), self.next_y, 1, self.ws, self.wr).wait_send()
                copy(self.far(), self.next_x, 3, self.ws, self.wr).wait_send()
                copy(self.far(), self.partner, 1, self.qs, self.qr).wait_send()

            self.by_half(w, self.half, mine)
            self.by_half(w, 1 - self.half, lambda copy: copy(
                self.near(), None, self.partner, 2, self.qs, self.qr).wait_send())
            self.by_share(w, self.half, self.core, mine_far)
            self.by_share(w, 1 - self.half, self.core, lambda copy: copy(
                self.far(), self.partner, 3, self.qs, self.qr).wait_send())


class Switch:
    def __init__(self, out, taken, send, recv):
        self.out, self.taken, self.send, self.recv = out, taken, send, recv
        self.dp, self.seq = lax.axis_index("dp"), lax.axis_index("seq")

    def copy(self, half, k):
        to = lax.rem(self.seq + k, 32)
        return pltpu.make_async_remote_copy(
            src_ref=self.out.at[half, to], dst_ref=self.taken.at[half, self.seq],
            send_sem=self.send.at[half, k], recv_sem=self.recv.at[half, k],
            device_id=(self.dp, to), device_id_type=MESH)

    def start(self, half):
        @pl.loop(1, 32)
        def _(k):
            self.copy(half, k).start()

        self.taken[half, self.seq] = self.out[half, self.seq]

    def wait(self, half):
        @pl.loop(1, 32)
        def _(k):
            block = self.taken.at[half, lax.rem(self.seq - k + 32, 32)]
            pltpu.make_async_remote_copy(
                src_ref=block, dst_ref=block, send_sem=self.send.at[half, k], recv_sem=self.recv.at[half, k],
                device_id=(self.dp, lax.rem(self.seq + k, 32)), device_id_type=MESH).wait_recv()

    def drain(self):
        for half in range(2):
            @pl.loop(1, 32)
            def _(k):
                self.copy(half, k).wait_send()


class Reduce:
    def __init__(self, theirs, ours, taken, pieces, plane, total, z_out, z_in, x_out, x_in, sems):
        self.theirs, self.ours, self.taken, self.pieces, self.plane = theirs, ours, taken, pieces, plane
        self.total, self.z_out, self.z_in, self.x_out, self.x_in = total, z_out, z_in, x_out, x_in
        (self.cs, self.cr, self.ps, self.pr, self.zs, self.zr, self.xs, self.xr) = sems
        self.core, self.x, self.y, self.z = place()
        self.holds = jnp.logical_and(self.x < 3, lax.div(self.y, 2) == self.core)
        self.me = self.x * 4 + self.y

    def core_copy(self, part):
        return pltpu.make_async_remote_copy(
            src_ref=self.theirs.at[part], dst_ref=self.taken.at[part],
            send_sem=self.cs.at[part], recv_sem=self.cr.at[part],
            device_id=device(1 - self.core, self.x, self.y, self.z), device_id_type=MESH)

    def core_start(self, mixed_t, grad):
        half = times(mixed_t[1 - self.core], grad)
        for part in range(2):
            for upper in range(2):
                at = 144 * upper + 72 * part
                self.theirs[part, upper] = half[at:at + 72].astype(BF16)
            self.core_copy(part).start()
        half = times(mixed_t[self.core], grad)
        for part in range(2):
            for upper in range(2):
                at = 144 * upper + 72 * part
                self.ours[part, upper] = half[at:at + 72]

    def plane_copy(self, part, k):
        piece = lax.rem(k + self.x + 2 * self.y, 6)
        upper, x = lax.div(piece, 3), lax.rem(piece, 3)
        mine = jnp.logical_and(self.x == x, self.y == self.core * 2 + upper)
        copy = pltpu.make_async_remote_copy(
            src_ref=self.pieces.at[part, upper, x], dst_ref=self.plane.at[part, self.me],
            send_sem=self.ps.at[part, k], recv_sem=self.pr.at[part, self.me],
            device_id=device(self.core, x, self.core * 2 + upper, self.z), device_id_type=MESH)
        return mine, copy

    def plane_start(self, part):
        self.core_copy(part).wait_recv()
        for upper in range(2):
            for x in range(3):
                columns = slice(384 * x, 384 * x + 384)
                self.pieces[part, upper, x] = (
                    self.ours[part, upper, :, columns]
                    + self.taken[part, upper, :, columns].astype(F32)).astype(BF16)

        @pl.loop(0, 6)
        def _(k):
            mine, copy = self.plane_copy(part, k)
            pl.when(jnp.logical_not(mine))(copy.start)

        @pl.when(self.holds)
        def _():
            self.plane[part, self.me] = self.pieces[part, lax.rem(self.y, 2), self.x]

    def z_copy(self, part, k):
        k = lax.rem(k + self.z, 8)
        block = 4 * part + lax.rem(k, 4)
        to = lax.div(k, 4) * 8 + block
        return to != self.z, pltpu.make_async_remote_copy(
            src_ref=self.z_out.at[block], dst_ref=self.z_in.at[self.z],
            send_sem=self.zs.at[part, k], recv_sem=self.zr.at[self.z],
            device_id=device(self.core, self.x, self.y, to), device_id_type=MESH)

    def z_start(self, part):
        @pl.when(self.holds)
        def _():
            @pl.loop(0, 16)
            def _(k):
                @pl.when(k != self.me)
                def _():
                    block = self.plane.at[part, k]
                    pltpu.make_async_remote_copy(
                        src_ref=block, dst_ref=block, send_sem=self.ps.at[part, 0], recv_sem=self.pr.at[part, k],
                        device_id=device(1 - self.core, self.x, self.y, self.z), device_id_type=MESH).wait_recv()

            for r in range(3):
                rows = slice(24 * r, 24 * r + 24)
                sum_rows = self.plane[part, 0, rows].astype(F32)
                for k in range(1, 16):
                    sum_rows = sum_rows + self.plane[part, k, rows].astype(F32)
                self.total[rows] = sum_rows
            for k in range(4):
                self.z_out[4 * part + k] = self.total[18 * k:18 * k + 18, :].astype(BF16)

            @pl.loop(0, 8)
            def _(k):
                away, copy = self.z_copy(part, k)
                pl.when(away)(copy.start)

            @pl.when(lax.div(lax.rem(self.z, 8), 4) == part)
            def _():
                self.z_in[self.z] = self.z_out[lax.rem(self.z, 8)]

    def x_copy(self, k):
        other = lax.div(k, 4)
        return pltpu.make_async_remote_copy(
            src_ref=self.x_out, dst_ref=self.x_in.at[self.x],
            send_sem=self.xs.at[k], recv_sem=self.xr.at[self.x],
            device_id=device(lax.rem(self.core + other, 2), lax.rem(self.x + k, 4), self.y, self.z),
            device_id_type=MESH)

    def x_start(self):
        @pl.when(self.holds)
        def _():
            @pl.loop(0, 16)
            def _(k):
                @pl.when(k != self.z)
                def _():
                    block = self.z_in.at[k]
                    pltpu.make_async_remote_copy(
                        src_ref=block, dst_ref=block, send_sem=self.zs.at[0, 0], recv_sem=self.zr.at[k],
                        device_id=device(1 - self.core, self.x, self.y, self.z), device_id_type=MESH).wait_recv()

            sum_rows = self.z_in[0].astype(F32)
            for k in range(1, 16):
                sum_rows = sum_rows + self.z_in[k].astype(F32)
            self.x_out[...] = sum_rows.astype(BF16)

            @pl.loop(1, 8)
            def _(k):
                self.x_copy(k).start()

            self.x_in[self.x] = self.x_out[...]

    def finish(self, out):
        for k in range(3):
            @pl.when(jnp.logical_not(jnp.logical_and(self.holds, self.x == k)))
            def _():
                block = self.x_in.at[k]
                pltpu.make_async_remote_copy(
                    src_ref=block, dst_ref=block, send_sem=self.xs.at[0], recv_sem=self.xr.at[k],
                    device_id=device(1 - self.core, self.x, self.y, self.z), device_id_type=MESH).wait_recv()
            out[:, 384 * k:384 * k + 384] = self.x_in[k].astype(F32)

    def drain(self):
        for part in range(2):
            self.core_copy(part).wait_send()

            @pl.loop(0, 6)
            def _(k):
                mine, copy = self.plane_copy(part, k)
                pl.when(jnp.logical_not(mine))(copy.wait_send)

        @pl.when(self.holds)
        def _():
            for part in range(2):
                @pl.loop(0, 8)
                def _(k):
                    away, copy = self.z_copy(part, k)
                    pl.when(away)(copy.wait_send)

            @pl.loop(1, 8)
            def _(k):
                self.x_copy(k).wait_send()


REDUCE_SCRATCH = [
    pltpu.VMEM((2, 2, 72, 1152), BF16),
    pltpu.VMEM((2, 2, 72, 1152), F32),
    pltpu.VMEM((2, 2, 72, 1152), BF16),
    pltpu.VMEM((2, 2, 3, 72, 384), BF16),
    pltpu.VMEM((2, 16, 72, 384), BF16),
    pltpu.VMEM((72, 384), F32),
    pltpu.VMEM((8, 18, 384), BF16),
    pltpu.VMEM((16, 18, 384), BF16),
    pltpu.VMEM((18, 384), BF16),
    pltpu.VMEM((3, 18, 384), BF16),
]
REDUCE_SEMS = [pltpu.SemaphoreType.DMA(n) for n in ((2,), (2,), (2, 6), (2, 16), (2, 8), (16,), (8,), (3,))]


def times(left, right):
    return jnp.dot(left, right, preferred_element_type=F32)


def times_transposed(left, right):
    return lax.dot_general(left, right, (((1,), (1,)), ((), ())), preferred_element_type=F32)


def transposed_times(left, right):
    return lax.dot_general(left, right, (((0,), (0,)), ((), ())), preferred_element_type=F32)


def split_heads(ref, array):
    for h in range(HEADS):
        ref[h] = array[HEAD * h:HEAD * h + HEAD, :]


def attend(head, queries, keys, values, visible, weights, out):
    scores = transposed_times(keys[head], queries[head]) * SCALE
    if visible is not None:
        scores = jnp.where(visible, scores, -1e30)
    powers = jnp.exp(scores - jnp.max(scores, axis=0, keepdims=True))
    share = powers / jnp.sum(powers, axis=0, keepdims=True)
    weights[head] = share
    out[head] = times(values[head], share.astype(BF16)).astype(BF16)


def attend_grad(head, upstream, queries, keys, values, weights, query_grad, key_grad, value_grad):
    upper, share = upstream[head], weights[head]
    share_grad = transposed_times(values[head], upper)
    score_grad = (share * (share_grad - jnp.sum(share_grad * share, axis=0, keepdims=True))).astype(BF16)
    query_grad[head] = (SCALE * times(keys[head], score_grad)).astype(BF16)
    if key_grad is not None:
        value_grad[head] = times_transposed(upper, share.astype(BF16)).astype(BF16)
        key_grad[head] = (SCALE * times_transposed(queries[head], score_grad)).astype(BF16)


def each_head(go):
    for h in range(HEADS):
        go(h)


def block_pair(
    tokens_in, qkv_in, text_in, length, w_os, w_qc, w_oc, w_qkv, cotangent_in,
    heads_out, tokens_grad, qkv_grad, os_grad, *scratch,
):
    tokens, qkv, text, cotangent, brought = scratch[-5:]
    fetch = [pltpu.make_async_copy(source, target, brought.at[k]) for k, (source, target) in enumerate(
        ((qkv_in, qkv), (tokens_in, tokens), (text_in, text), (cotangent_in, cotangent)))]
    for copy in fetch:
        copy.start()
    full, landing, sems, scratch = scratch[0:6], scratch[6:12], scratch[12:20], scratch[20:]
    (to_patches, from_frames, to_frames, from_patches, s1_send, s1_recv, s2_send, s2_recv,
     spatial_w, cross_w, temporal_w, mixed_heads, mixed_t, cross_queries, cross_heads, cross_up, upstream,
     temporal, temporal_up, temporal_heads, temporal_grads, wide_t, half_t, hidden_ref) = scratch[0:24]
    g = Gather((w_os, w_qc, w_oc, w_qkv), landing, full, sems)
    forth = Switch(to_patches, from_frames, s1_send, s1_recv)
    back = Switch(to_frames, from_patches, s2_send, s2_recv)
    r = Reduce(*scratch[24:34], scratch[34:42])

    barrier = pltpu.get_barrier_semaphore()
    roll = Roll(scratch[42])
    greeted = roll.greet(barrier)
    for b in WEIGHTS:
        g.stage(b)
    pl.semaphore_wait(barrier, greeted)

    def whole(w):
        return full[w][...].reshape(-1, COLUMNS[w])

    def join(heads, into=wide_t):
        for h in range(HEADS):
            into[HEAD * h:HEAD * h + HEAD, :] = heads[h]
        return into[...].T

    def in_halves(transposed, array):
        row = lax.broadcasted_iota(jnp.int32, (128, 128), 0)
        token = lax.broadcasted_iota(jnp.int32, (128, 128), 1)
        if transposed:
            row, token = token, row
        from_row = 4 * lax.div(lax.rem(row, 64), 2) + 2 * lax.div(row, 64) + lax.rem(row, 2)
        moves = jnp.where(from_row == token, 1.0, 0.0).astype(BF16)
        return times(moves, array).astype(BF16)

    def spatial_pair(i):
        for h in (2 * i, 2 * i + 1):
            attend(h, qkv.at[0], qkv.at[1], qkv.at[2], None, spatial_w, mixed_heads)

    for w in (OS, QC, OC):
        g.z_start(w)
    roll.call(0)
    fetch[0].wait()
    for s in range(3):
        spatial_pair(s)
        for w in (OS, QC, OC):
            g.z_step(w, s)
        roll.call(s + 1)
        if s == 1:
            g.z_start(TQ)
    g.z_start(TK)
    g.z_start(TV)
    spatial_pair(3)
    mixed = join(mixed_heads)
    mixed_in_halves = in_halves(False, mixed).T
    for half in range(2):
        mixed_t[half] = mixed_in_halves[288 * half:288 * half + 288, :]
    for copy in fetch[1:]:
        copy.wait()
    for w in (OS, QC, OC):
        g.z_step(w, 3)
    g.z_finish(OS)
    g.pack(OS)
    g.z_finish(QC)
    g.pack(QC)
    g.z_finish(OC)
    g.pack(OC)
    roll.call(4)
    for w in (TQ, TK, TV):
        g.z_step(w, 0)
    g.y_step(OS)
    for w in (TQ, TK, TV):
        g.z_step(w, 1)
    g.y_step(QC)
    roll.call(5)
    g.y_last(OS)
    g.y_step(OC)
    g.x_step(OS)
    roll.call(6)
    g.z_step(TQ, 2)
    g.y_last(QC)
    g.z_step(TK, 2)
    g.x_step(QC)
    roll.call(7)
    g.z_step(TV, 2)
    g.x_last(OS)
    g.y_last(OC)
    g.z_step(TQ, 3)
    g.z_finish(TQ)
    g.pack(TQ)
    g.x_step(OC)
    g.x_last(QC)
    g.finish(OS)
    hidden = (tokens[...].astype(F32) + times(mixed, whole(OS))).astype(BF16)
    hidden = in_halves(False, hidden)
    hidden_ref[...] = hidden
    for w in (TK, TV):
        g.z_step(w, 3)
        g.z_finish(w)
        g.pack(w)
    g.finish(QC)
    roll.call(8)
    g.x_last(OC)
    queries = times(hidden, whole(QC)).astype(BF16)
    g.y_step(TQ)
    seen = lax.broadcasted_iota(jnp.int32, (128, 64), 0) < length[0]
    for half in range(2):
        split_heads(cross_queries.at[half], queries[64 * half:64 * half + 64, :].T)
        each_head(lambda h: attend(
            h, cross_queries.at[half], text.at[0], text.at[1], seen, cross_w.at[half], cross_heads.at[half]))
    g.finish(OC)
    for half in range(2):
        after = (hidden_ref[64 * half:64 * half + 64, :].astype(F32)
                 + times(join(cross_heads.at[half], half_t), whole(OC))).astype(BF16)
        to_patches[half] = after.reshape(32, 2, 1152)
        forth.start(half)
    g.y_step(TK)
    g.y_last(TQ)
    g.x_step(TQ)
    g.y_step(TV)
    g.y_last(TK)
    g.x_last(TQ)
    g.x_step(TK)
    g.y_last(TV)
    g.x_step(TV)
    g.x_last(TK)
    g.x_last(TV)
    for half in range(2):
        split_heads(temporal_up.at[half], cotangent[:, 2 * half:2 * half + 2, :].reshape(64, 576).T)
    for w in (TQ, TK, TV):
        g.finish(w)

    same = (lax.rem(lax.broadcasted_iota(jnp.int32, (64, 64), 0), 2)
            == lax.rem(lax.broadcasted_iota(jnp.int32, (64, 64), 1), 2))
    for half in range(2):
        forth.wait(half)
        patched = from_frames[half].reshape(64, 1152)
        for i, w in enumerate((TQ, TK, TV)):
            split_heads(temporal.at[i], times(patched, whole(w)).astype(BF16).T)
        for h in range(HEADS):
            attend(h, temporal.at[0], temporal.at[1], temporal.at[2], same, temporal_w, temporal_heads.at[half])
            attend_grad(h, temporal_up.at[half], temporal.at[0], temporal.at[1], temporal.at[2], temporal_w,
                        temporal_grads.at[0], temporal_grads.at[1], temporal_grads.at[2])
        patch_grad = times_transposed(join(temporal_grads.at[0], half_t), whole(TQ))
        for i, w in ((1, TK), (2, TV)):
            patch_grad = patch_grad + times_transposed(join(temporal_grads.at[i], half_t), whole(w))
        to_frames[half] = patch_grad.astype(BF16).reshape(32, 2, 1152)
        back.start(half)
    for half in range(2):
        heads_out[:, 2 * half:2 * half + 2, :] = join(temporal_heads.at[half], half_t).reshape(32, 2, 576)
    g.drain()
    forth.drain()
    for half in range(2):
        back.wait(half)
        after_grad = from_patches[half].reshape(64, 1152)
        split_heads(cross_up, times_transposed(after_grad, whole(OC)).astype(BF16).T)
        each_head(lambda h: attend_grad(
            h, cross_up, cross_queries.at[half], text.at[0], text.at[1], cross_w.at[half], cross_heads.at[half],
            None, None))
        hidden_ref[64 * half:64 * half + 64, :] = (
            after_grad.astype(F32) + times_transposed(join(cross_heads.at[half], half_t), whole(QC))).astype(BF16)
    hidden_grad = hidden_ref[...]
    r.core_start(mixed_t, hidden_grad)
    split_heads(upstream, in_halves(True, times_transposed(hidden_grad, whole(OS)).astype(BF16)).T)
    r.plane_start(0)
    r.plane_start(1)
    tokens_grad[...] = in_halves(True, hidden_ref[...])
    each_head(lambda h: attend_grad(
        h, upstream, qkv.at[0], qkv.at[1], qkv.at[2], spatial_w, qkv_grad.at[0], qkv_grad.at[1],
        qkv_grad.at[2]))
    r.z_start(0)
    r.z_start(1)
    r.x_start()
    r.finish(os_grad)
    back.drain()
    r.drain()


def hand_on(*refs):
    for k in range(4):
        refs[4 + k][...] = refs[k][...]


def shards(tokens, spatial_qkv, text_kv, text_len, w_os, w_qc, w_oc, w_qkv, cotangent):
    heads = (HEADS, HEAD, 128)
    vmem = pl.BlockSpec(memory_space=pltpu.VMEM)
    dma = pltpu.SemaphoreType.DMA
    anywhere = pl.BlockSpec(memory_space=pl.ANY)
    results = pl.pallas_call(
        block_pair,
        out_shape=[
            jax.ShapeDtypeStruct((32, 4, 576), BF16),
            jax.ShapeDtypeStruct((128, 1152), BF16),
            jax.ShapeDtypeStruct((3,) + heads, BF16),
            jax.ShapeDtypeStruct((18, 1152), F32),
        ],
        in_specs=[anywhere] * 3 + [pl.BlockSpec(memory_space=pltpu.SMEM)] + [vmem] * 4 + [anywhere],
        out_specs=[vmem] * 4,
        scratch_shapes=[pltpu.VMEM((4, 8 * rows, columns), BF16) for rows, columns in zip(ROWS, COLUMNS)]
        + [pltpu.VMEM((8, rows, columns), BF16) for rows, columns in zip(ROWS, COLUMNS)]
        + [dma((6, 4))] * 8
        + [pltpu.VMEM((2, 32, 2, 1152), BF16)] * 4 + [dma((2, 32))] * 4
        + [pltpu.VMEM((HEADS, 128, 128), F32), pltpu.VMEM((2, HEADS, 128, 64), F32), pltpu.VMEM((HEADS, 64, 64), F32)]
        + [pltpu.VMEM(heads, BF16), pltpu.VMEM((2, 288, 128), BF16)]
        + [pltpu.VMEM((2, HEADS, HEAD, 64), BF16)] * 2 + [pltpu.VMEM((HEADS, HEAD, 64), BF16), pltpu.VMEM(heads, BF16)]
        + [pltpu.VMEM((k, HEADS, HEAD, 64), BF16) for k in (3, 2, 2, 3)]
        + [pltpu.VMEM((576, 128), BF16), pltpu.VMEM((576, 64), BF16), pltpu.VMEM((128, 1152), BF16)]
        + REDUCE_SCRATCH + REDUCE_SEMS + [pltpu.SemaphoreType.REGULAR((8,))]
        + [pltpu.VMEM((128, 1152), BF16), pltpu.VMEM((3,) + heads, BF16), pltpu.VMEM((2,) + heads, BF16),
           pltpu.VMEM((32, 4, 576), BF16), dma((4,))],
        compiler_params=pltpu.CompilerParams(
            collective_id=0, has_side_effects=True, vmem_limit_bytes=56 * 2**20),
        name="block_pair",
    )(
        tokens.reshape(128, 1152),
        jnp.transpose(spatial_qkv[0, 0], (1, 2, 0)).reshape((3,) + heads),
        jnp.transpose(text_kv[0], (1, 2, 0)).reshape((2,) + heads),
        text_len, w_os, w_qc, w_oc, w_qkv,
        cotangent.reshape(32, 4, 576),
    )
    temporal_heads, tokens_grad, qkv_grad, os_grad = pl.pallas_call(
        hand_on,
        out_shape=[jax.ShapeDtypeStruct(r.shape, r.dtype) for r in results],
        in_specs=[vmem] * 4,
        out_specs=[vmem] * 4,
        name="hand_on",
    )(*results)
    return (
        temporal_heads[None],
        tokens_grad[None, None],
        jnp.transpose(qkv_grad.reshape(3, 576, 128), (2, 0, 1))[None, None],
        os_grad,
    )


def solution(mesh):
    placed = (
        P("dp", "seq", None, None),
        P("dp", "seq", None, None, None),
        P("dp", None, None, None),
        P("dp"),
        P("seq", None),
        P("seq", None),
        P("seq", None),
        P("seq", None),
        P("dp", None, "seq", None),
    )
    return jax.shard_map(
        shards,
        mesh=mesh,
        in_specs=placed,
        out_specs=(
            P("dp", None, "seq", None),
            P("dp", "seq", None, None),
            P("dp", "seq", None, None, None),
            P("seq", None),
        ),
        check_vma=False,
    )
```
